128 devices in a mesh: gx: 16 (over y, x), gy: 8 (over z, core).
Axes of the slice: x: 4, y: 4, z: 4, core: 2. Of those that a mesh axis runs over, the one named last changes fastest.
Arguments:
- point_features: float32 [64, 2097152], P(None, ('gx', 'gy')), may hold values from -6 to 6
- neighbour_rows: int32 [4, 64, 64, 256], P(None, 'gx', 'gy'), may hold values from 0 to 16383
- neighbour_owner: int32 [4, 64, 64, 256], P(None, 'gx', 'gy'), may hold values from 0 to 127, as said below
- valid: int32 [4, 64, 64, 256], P(None, 'gx', 'gy'), may hold values from 0 to 1
- proj: bfloat16 [64, 64], replicated, may hold values from -0.75 to 0.75
- kernel_one: bfloat16 [64, 64, 3, 3, 3], replicated, may hold values from -0.15625 to 0.15625
- kernel_two: bfloat16 [64, 64, 3, 3, 3], replicated, may hold values from -0.15625 to 0.15625
- cotangent: bfloat16 [64, 64, 64, 256], P(None, 'gx', 'gy'), may hold values from -6 to 6
Outputs:
- point_grad: float32 [64, 2097152], P(None, ('gx', 'gy'))
The draws below stay inside these ranges and needn't reach their ends.
Inputs may be any that keep to these rules, and one draw needn't show every extreme that they name: `neighbour_owner`: owner device (flat index along gx+gy) of a slot's point. Among the valid slots of the cells of one device, at most 256 name any one owner, in any arrangement over the slots, and on every device some owner is named by exactly 256 valid slots.
All inputs are finite; a program needn't handle non-finite values.
Results may differ from the reference program's by a relative error of at most 0.0049.
Values may be sent and summed in bfloat16 or wider, within the bound.
A program may use at most 128 MiB of HBM per device.

```python
import jax
import jax.numpy as jnp
from jax import lax

C = 64
CX = 4
CY = 8
NZ = 256
K = 4
PTS_DEV = 16384
NX = 64
NY = 64
PTS = 2097152
SLOTS = 256
N_GY = 8
DEVICES = 128


def layout_slots(key):
    grid_shape = (K, NX, NY, NZ)
    edge_total = K * CX * CY * NZ
    k_index = lax.broadcasted_iota(jnp.int32, grid_shape, 0)
    x_index = lax.broadcasted_iota(jnp.int32, grid_shape, 1)
    y_index = lax.broadcasted_iota(jnp.int32, grid_shape, 2)
    z_index = lax.broadcasted_iota(jnp.int32, grid_shape, 3)
    device_index = x_index // CX * N_GY + y_index // CY
    edge_index = ((k_index * CX + x_index % CX) * CY + y_index % CY) * NZ + z_index
    shuffle_keys = jax.random.split(jax.random.fold_in(key, 105), DEVICES)
    shuffles = jax.vmap(lambda subkey: jax.random.permutation(subkey, edge_total))(shuffle_keys).astype(jnp.int32)
    shuffled = shuffles[device_index, edge_index]
    block_index = shuffled // SLOTS
    subkeys = jax.random.split(jax.random.fold_in(key, 101), DEVICES)
    tables = jax.vmap(lambda subkey: jax.random.permutation(subkey, DEVICES))(subkeys).astype(jnp.int32)
    owner_table = tables[device_index, block_index]
    density = jax.random.randint(jax.random.fold_in(key, 102), (DEVICES,), 20, 91)
    full_block = jax.random.randint(jax.random.fold_in(key, 103), (DEVICES,), 0, DEVICES)
    coin_draw = jax.random.randint(jax.random.fold_in(key, 104), grid_shape, 0, 100)
    usable = (coin_draw < density[device_index]) | (block_index == full_block[device_index])
    stray = jax.random.randint(jax.random.fold_in(key, 106), grid_shape, 0, DEVICES).astype(jnp.int32)
    owner = jnp.where(usable, owner_table, stray).astype(jnp.int32)
    return (owner, usable.astype(jnp.int32))


def draw_neighbour_owner(key, part):
    shared = layout_slots(key)
    return shared[0]


def draw_valid(key, part):
    shared = layout_slots(key)
    return shared[1]


def set_ends(entries, stream_key, smallest, largest):
    shape = entries.shape
    index_at = [jax.random.randint(jax.random.fold_in(stream_key, axis), (), 0, shape[axis]) for axis in range(len(shape))]
    entries = entries.at[tuple(index_at)].set(smallest)
    longest = shape.index(max(shape))
    index_at[longest] = (index_at[longest] + 1) % shape[longest]
    return entries.at[tuple(index_at)].set(largest)


def levels(own_key, extent, cuts, low, top_value):
    def one(dim, parts):
        heights = jax.random.uniform(jax.random.fold_in(jax.random.fold_in(own_key, 6), dim), (parts,), jnp.float32, low / len(cuts), top_value / len(cuts))
        return jnp.repeat(jnp.exp(heights), extent[dim] // parts).reshape((-1,) + (1,) * (len(extent) - dim - 1))

    loudness = one(*cuts[0])
    for cut in cuts[1:]:
        loudness = loudness * one(*cut)
    return loudness


def noise(key, extent, spread, most, pieces=(), dtype=jnp.bfloat16):
    loudness = levels(key, extent, pieces, -0.22, 0.18) if pieces else 1.0
    values = jax.random.normal(key, extent, jnp.float32) * spread * loudness
    return jnp.minimum(jnp.maximum(values, -most), most).astype(dtype)


def setup_inputs(seed: int = 0) -> dict:
    splits = jax.random.split(jax.random.key(seed), 9)
    return {
        "point_features": noise(splits[0], (C, PTS), 1.0, 6.0, ((1, 128),), jnp.float32),
        "neighbour_rows": set_ends(jax.random.randint(splits[1], (K, NX, NY, NZ), 0, PTS_DEV), jax.random.fold_in(splits[1], 1), 0, PTS_DEV - 1).astype(jnp.int32),
        "neighbour_owner": draw_neighbour_owner(jax.random.fold_in(splits[8], 71), 0),
        "valid": draw_valid(jax.random.fold_in(splits[8], 71), 0),
        "proj": noise(splits[4], (C, C), C ** -0.5, 0.75),
        "kernel_one": noise(splits[5], (C, C, 3, 3, 3), (27 * C) ** -0.5, 0.15625),
        "kernel_two": noise(splits[6], (C, C, 3, 3, 3), (27 * C) ** -0.5, 0.15625),
        "cotangent": noise(splits[7], (C, NX, NY, NZ), 1.0, 6.0, ((1, 16), (2, 8))),
    }


SCALE_ROOT = 0.7978845608
CUBIC_TERM = 0.044715


def gelu_slope(value):
    inner = SCALE_ROOT * (value + CUBIC_TERM * value * value * value)
    tangent = jnp.tanh(inner)
    return 0.5 * (1.0 + tangent) + 0.5 * value * (1.0 - tangent * tangent) * SCALE_ROOT * (1.0 + 3.0 * CUBIC_TERM * value * value)


def convolve(padded, kernel):
    result = lax.conv_general_dilated(padded.astype(jnp.float32)[None], kernel.astype(jnp.float32), (1, 1, 1), "VALID", dimension_numbers=("NCDHW", "OIDHW", "NCDHW"), precision=lax.Precision.HIGHEST)
    return result[0]


def flipped(kernel):
    return jnp.flip(kernel, (2, 3, 4)).transpose(1, 0, 2, 3, 4)


def pad_grid(field):
    return jnp.pad(field, ((0, 0), (1, 1), (1, 1), (1, 1)))


def reference(point_features, neighbour_rows, neighbour_owner, valid, proj, kernel_one, kernel_two, cotangent):
    channels = point_features.shape[0]
    position = (neighbour_owner * PTS_DEV + neighbour_rows).astype(jnp.int32)
    weights = valid.astype(jnp.float32)
    divisor = jnp.maximum(jnp.sum(weights, axis=0), 1.0)
    gathered = jnp.zeros((channels, NX, NY, NZ), jnp.float32)
    for neighbour in range(K):
        gathered = gathered + jnp.take(point_features, position[neighbour], axis=1).astype(jnp.float32) * weights[neighbour]
    averaged = (gathered / divisor).astype(jnp.bfloat16)
    latent = jnp.dot(proj.T, averaged.reshape(channels, -1), preferred_element_type=jnp.float32).astype(jnp.bfloat16).reshape(channels, NX, NY, NZ)
    preact = convolve(pad_grid(latent), kernel_one)
    upstream = convolve(pad_grid(cotangent), flipped(kernel_two))
    gated_grad = (upstream * gelu_slope(preact)).astype(jnp.bfloat16)
    latent_grad = convolve(pad_grid(gated_grad), flipped(kernel_one)).astype(jnp.bfloat16)
    projected = jnp.dot(proj, latent_grad.reshape(channels, -1), preferred_element_type=jnp.float32)
    cell_grad = projected / divisor.reshape(-1)
    point_grad = jnp.zeros((channels, PTS), jnp.float32)
    for neighbour in range(K):
        point_grad = point_grad.at[:, position[neighbour].reshape(-1)].add(cell_grad * weights[neighbour].reshape(-1))
    return point_grad
```

```python
import functools

import jax
import jax.numpy as jnp
from jax import lax
from jax.experimental import pallas as pl
from jax.experimental.pallas import tpu as pltpu
from jax.sharding import PartitionSpec as P

MESH = pl.DeviceIdType.MESH
SCALE_ROOT = 0.7978845608
CUBIC_TERM = 0.044715
LANES = 128
SPARE = 128
F32, BF16, I32 = jnp.float32, jnp.bfloat16, jnp.int32


def whole(space=pltpu.VMEM):
    return pl.BlockSpec(memory_space=space)


def params(mebibytes=60, **more):
    return pltpu.CompilerParams(vmem_limit_bytes=mebibytes * 1024 * 1024, **more)


def left_lanes(rows=1):
    return lax.broadcasted_iota(I32, (rows, LANES), 1) < LANES // 2


def route_kernel(owner_ref, rows_ref, valid_ref, slot_ref, want_ref, sums):
    blocks, width = owner_ref.shape
    owners, cap = want_ref.shape
    trash = owners * cap
    owner_of = lax.broadcasted_iota(I32, (owners, width), 0)
    rank_of = lax.broadcasted_iota(I32, (cap, width), 0)
    first = lax.broadcasted_iota(I32, (width, 2 * width), 0)
    second = lax.broadcasted_iota(I32, (width, 2 * width), 1)
    earlier = jnp.where((second >= width) | (first < second), 1.0, 0.0).astype(BF16)
    sums[...] = jnp.zeros_like(sums)

    def body(block, offset):
        owner = owner_ref[pl.ds(block, 1), :]
        rows = rows_ref[pl.ds(block, 1), :]
        used = valid_ref[pl.ds(block, 1), :] > 0
        hit = owner_of == jnp.where(used, owner, -1)
        counts = jnp.dot(jnp.where(hit, 1.0, 0.0).astype(BF16), earlier, preferred_element_type=F32)
        before = counts[:, :width] + offset
        rank = jnp.sum(jnp.where(hit, before, 0.0), axis=0, keepdims=True).astype(I32)
        place = (rank >> 7) * (owners * LANES) + owner * LANES + (rank & 127)
        slot_ref[pl.ds(block, 1), :] = jnp.where(used, place, trash)
        high = ((rows >> 7) + 1).astype(F32)
        low = (rows & 127).astype(F32)
        pieces = jnp.concatenate(
            [jnp.where(hit, high, 0.0).astype(BF16), jnp.where(hit, low, 0.0).astype(BF16)], axis=0
        )
        at_rank = jnp.where(rank_of == rank, 1.0, 0.0).astype(BF16)
        sums[...] += lax.dot_general(
            pieces, at_rank, (((1,), (1,)), ((), ())), preferred_element_type=F32
        )
        return offset + counts[:, width:]

    lax.fori_loop(0, blocks, body, jnp.zeros((owners, width), F32), unroll=2)
    want_ref[...] = (sums[:owners, :] * 128.0 + sums[owners:, :]).astype(I32)


def route(owner, rows, valid, owners, cap):
    blocks, width = owner.shape
    return pl.pallas_call(
        route_kernel,
        out_shape=(
            jax.ShapeDtypeStruct((blocks, width), I32),
            jax.ShapeDtypeStruct((owners, cap), I32),
        ),
        in_specs=[whole()] * 3,
        out_specs=(whole(), whole()),
        scratch_shapes=[pltpu.VMEM((2 * owners, cap), F32)],
        compiler_params=params(),
        name="route",
    )(owner, rows, valid)


def serve_kernel(asked_ref, features_ref, out_ref, table, stage):
    step = pl.program_id(0)
    per_step = out_ref.shape[0]
    points = features_ref.shape[1]

    @pl.when(step == 0)
    def _():
        table[:SPARE, :] = jnp.zeros((SPARE, LANES), F32)

        def fill(block, carry):
            at = pl.multiple_of(block * LANES, LANES)
            part = features_ref[:, pl.ds(at, LANES)]
            table[pl.ds(SPARE + at, LANES), :] = jnp.concatenate([part, part], axis=0).T
            return carry

        lax.fori_loop(0, points // LANES, fill, 0, unroll=2)

    left = left_lanes()
    for part in range(per_step):
        source = step * per_step + part

        def gather(group, carry):
            for u in range(32):
                row = group * 32 + u
                one = table[pl.ds(asked_ref[source, row], 1), :]
                two = table[pl.ds(asked_ref[source, row + LANES], 1), :]
                stage[pl.ds(row, 1), :] = jnp.where(left, one, two)
            return carry

        lax.fori_loop(0, LANES // 32, gather, 0)
        out_ref[part] = stage[...].astype(BF16)


def serve(asked, features):
    sources, cap = asked.shape
    points = features.shape[1]
    per_step = 4
    return pl.pallas_call(
        serve_kernel,
        grid=(sources // per_step,),
        out_shape=jax.ShapeDtypeStruct((sources, LANES, LANES), BF16),
        in_specs=[whole(pltpu.SMEM), whole()],
        out_specs=pl.BlockSpec((per_step, LANES, LANES), lambda s: (s, 0, 0)),
        scratch_shapes=[
            pltpu.VMEM((SPARE + points, LANES), F32),
            pltpu.VMEM((LANES, LANES), F32),
        ],
        compiler_params=params(),
        name="serve",
    )(asked, features)


def column_of(row):
    return jnp.broadcast_to(row, (LANES, row.shape[1])).T


def collect_kernel(slot_ref, got_ref, share_ref, proj_ref, out_ref, table, stage):
    step = pl.program_id(0)
    strips = pl.num_programs(0)
    depth = slot_ref.shape[0] // strips
    half = got_ref.shape[0]
    cells = stage.shape[0]

    @pl.when(step == 0)
    def _():
        left = left_lanes(256)

        def fill(block, carry):
            at = pl.multiple_of(block * 256, 256)
            part = got_ref[pl.ds(at, 256), :].astype(F32)
            table[pl.ds(at, 256), :] = jnp.where(left, part, 0.0)
            table[pl.ds(half + at, 256), :] = jnp.where(left, 0.0, part)
            return carry

        lax.fori_loop(0, half // 256, fill, 0)
        table[2 * half :, :] = jnp.zeros((8, LANES), F32)

    def gather(group, carry):
        for u in range(16):
            cell = group * 16 + u
            rows = [table[pl.ds(slot_ref[k * strips + step, cell], 1), :] for k in range(depth)]
            stage[pl.ds(cell, 1), :] = (rows[0] + rows[1]) + (rows[2] + rows[3])
        return carry

    lax.fori_loop(0, cells // 16, gather, 0)
    total = stage[...]
    total = total + pltpu.roll(total, LANES // 2, 1)
    averaged = (total * column_of(share_ref[0])).astype(BF16)
    out_ref[0] = jnp.dot(averaged, proj_ref[...], preferred_element_type=F32).astype(BF16)


def collect(slot, got, share, proj):
    strips, _, cells = share.shape
    half = got.shape[0]
    return pl.pallas_call(
        collect_kernel,
        grid=(strips,),
        out_shape=jax.ShapeDtypeStruct((strips, cells, LANES), BF16),
        in_specs=[
            whole(pltpu.SMEM),
            whole(),
            pl.BlockSpec((1, 1, cells), lambda s: (s, 0, 0)),
            whole(),
        ],
        out_specs=pl.BlockSpec((1, cells, LANES), lambda s: (s, 0, 0)),
        scratch_shapes=[
            pltpu.VMEM((2 * half + 8, LANES), F32),
            pltpu.VMEM((cells, LANES), F32),
        ],
        compiler_params=params(),
        name="collect",
    )(slot, got, share, proj)


AROUND = ((1, 0), (-1, 0), (0, 1), (0, -1), (1, 1), (1, -1), (-1, 1), (-1, -1))


def exchange_kernel(
    size_x, size_y, rows_ref, out_ref, send_x, send_y, come_x, come_y, come_c, sent, come
):
    i, j = lax.axis_index("gx"), lax.axis_index("gy")
    nx, ny, cells, _ = rows_ref.shape
    left = left_lanes(cells)

    def device(di, dj):
        return (lax.rem(i + di + size_x, size_x), lax.rem(j + dj + size_y, size_y))

    barrier = pltpu.get_barrier_semaphore()
    for di, dj in AROUND:
        pl.semaphore_signal(barrier, inc=1, device_id=device(di, dj), device_id_type=MESH)
    pl.semaphore_wait(barrier, len(AROUND))

    for at, x in ((0, nx - 1), (1, 0)):
        for q in range(ny // 2):
            send_x[at, q] = jnp.where(left, rows_ref[x, 2 * q], rows_ref[x, 2 * q + 1])
    for at, y in ((0, ny - 1), (1, 0)):
        for q in range(nx // 2):
            send_y[at, q] = jnp.where(left, rows_ref[2 * q, y], rows_ref[2 * q + 1, y])
    copies = []
    for at, (di, dj) in enumerate(AROUND):
        if dj == 0:
            pair = (send_x.at[at], come_x.at[at])
        elif di == 0:
            pair = (send_y.at[at - 2], come_y.at[at - 2])
        else:
            pair = (
                rows_ref.at[nx - 1 if di > 0 else 0, ny - 1 if dj > 0 else 0],
                come_c.at[at - 4],
            )
        copies.append(
            pltpu.make_async_remote_copy(
                src_ref=pair[0],
                dst_ref=pair[1],
                send_sem=sent.at[at],
                recv_sem=come.at[at],
                device_id=device(di, dj),
                device_id_type=MESH,
            )
        )
        copies[-1].start()
    for x in range(nx):
        for y in range(ny):
            out_ref[x + 1, y + 1] = rows_ref[x, y]
    for copy in copies:
        copy.wait()

    def apart(ref, at, q):
        both = ref[at, q].astype(F32)
        turned = pltpu.roll(both, LANES // 2, 1)
        return jnp.where(left, both, turned), jnp.where(left, turned, both)

    inside_x = (i > 0, i < size_x - 1)
    inside_y = (j > 0, j < size_y - 1)
    for at, x in ((0, 0), (1, nx + 1)):
        for q in range(ny // 2):
            for p, row in enumerate(apart(come_x, at, q)):
                out_ref[x, 2 * q + p + 1] = jnp.where(inside_x[at], row, 0.0).astype(BF16)
    for at, y in ((0, 0), (1, ny + 1)):
        for q in range(nx // 2):
            for p, row in enumerate(apart(come_y, at, q)):
                out_ref[2 * q + p + 1, y] = jnp.where(inside_y[at], row, 0.0).astype(BF16)
    for at, (di, dj) in enumerate(AROUND[4:]):
        ax, ay = (0 if di > 0 else 1), (0 if dj > 0 else 1)
        keep = inside_x[ax] & inside_y[ay]
        row = jnp.where(keep, come_c[at].astype(F32), 0.0).astype(BF16)
        out_ref[0 if di > 0 else nx + 1, 0 if dj > 0 else ny + 1] = row


def exchange(rows, size_x, size_y):
    nx, ny, cells, _ = rows.shape
    return pl.pallas_call(
        functools.partial(exchange_kernel, size_x, size_y),
        out_shape=jax.ShapeDtypeStruct((nx + 2, ny + 2, cells, LANES), BF16),
        in_specs=[whole()],
        out_specs=whole(),
        scratch_shapes=[
            pltpu.VMEM((2, ny // 2, cells, LANES), BF16),
            pltpu.VMEM((2, nx // 2, cells, LANES), BF16),
            pltpu.VMEM((2, ny // 2, cells, LANES), BF16),
            pltpu.VMEM((2, nx // 2, cells, LANES), BF16),
            pltpu.VMEM((4, cells, LANES), BF16),
            pltpu.SemaphoreType.DMA((8,)),
            pltpu.SemaphoreType.DMA((8,)),
        ],
        compiler_params=params(collective_id=0, has_side_effects=True),
        name="exchange",
    )(rows)


def gelu_slope(value):
    inner = SCALE_ROOT * (value + CUBIC_TERM * value * value * value)
    tangent = jnp.tanh(inner)
    return 0.5 * (1.0 + tangent) + 0.5 * value * (1.0 - tangent * tangent) * SCALE_ROOT * (
        1.0 + 3.0 * CUBIC_TERM * value * value
    )


def taps_of(kernel):
    o, i = kernel.shape[:2]
    taps = kernel.transpose(2, 3, 1, 4, 0)
    taps = jnp.concatenate([taps, jnp.zeros((3, 1, i, 3, o), taps.dtype)], axis=1)
    return jnp.concatenate([taps, taps], axis=-1).reshape(12 * i, 6 * o)


def conv_strip(padded_ref, taps_ref, x, y):
    cells = padded_ref.shape[2]
    left = left_lanes(cells)
    parts = []
    for a in range(3):
        parts.append(jnp.where(left, padded_ref[x + a, y], padded_ref[x + a, y + 1]))
        parts.append(padded_ref[x + a, y + 2])
    sums = jnp.dot(jnp.concatenate(parts, axis=1), taps_ref[...], preferred_element_type=F32)
    depth = lax.broadcasted_iota(I32, (cells, LANES), 0)
    low = jnp.where(depth == 0, 0.0, pltpu.roll(sums[:, :LANES], 1, 0))
    high = jnp.where(depth == cells - 1, 0.0, pltpu.roll(sums[:, 2 * LANES :], cells - 1, 0))
    return sums[:, LANES : 2 * LANES] + low + high


def upstream_kernel(ny, padded_ref, taps_ref, out_ref):
    step = pl.program_id(0)
    out_ref[0] = conv_strip(padded_ref, taps_ref, step // ny, step % ny)


def gate_kernel(ny, padded_ref, taps_ref, upstream_ref, out_ref):
    step = pl.program_id(0)
    preact = conv_strip(padded_ref, taps_ref, step // ny, step % ny)
    out_ref[0] = (upstream_ref[0] * gelu_slope(preact)).astype(BF16)


def strip_spec(cells):
    return pl.BlockSpec((1, cells, LANES), lambda s: (s, 0, 0))


def conv_cost(strips, cells):
    return pl.CostEstimate(
        flops=2 * strips * cells * 12 * 64 * 6 * 64, bytes_accessed=12 << 20, transcendentals=0
    )


def upstream_of(padded, taps):
    nx, ny, cells = padded.shape[0] - 2, padded.shape[1] - 2, padded.shape[2]
    return pl.pallas_call(
        functools.partial(upstream_kernel, ny),
        grid=(nx * ny,),
        out_shape=jax.ShapeDtypeStruct((nx * ny, cells, LANES), F32),
        in_specs=[whole(), whole()],
        out_specs=strip_spec(cells),
        compiler_params=params(),
        cost_estimate=conv_cost(nx * ny, cells),
        name="upstream",
    )(padded, taps)


def gated(padded, taps, upstream):
    nx, ny, cells = padded.shape[0] - 2, padded.shape[1] - 2, padded.shape[2]
    return pl.pallas_call(
        functools.partial(gate_kernel, ny),
        grid=(nx * ny,),
        out_shape=jax.ShapeDtypeStruct((nx * ny, cells, LANES), BF16),
        in_specs=[whole(), whole(), strip_spec(cells)],
        out_specs=strip_spec(cells),
        compiler_params=params(),
        cost_estimate=conv_cost(nx * ny, cells),
        name="gated",
    )(padded, taps, upstream)


def spread_kernel(ny, slot_ref, padded_ref, taps_ref, proj_ref, share_ref, out_ref, slots, stage):
    step = pl.program_id(0)
    strips = pl.num_programs(0)
    depth = slot_ref.shape[0] // strips
    half = out_ref.shape[0]
    cells = stage.shape[0]

    @pl.when(step == 0)
    def _():
        def clear(block, carry):
            slots[pl.ds(pl.multiple_of(block * 256, 256), 256), :] = jnp.zeros((256, LANES), F32)
            return carry

        lax.fori_loop(0, 2 * half // 256, clear, 0)

    latent_grad = conv_strip(padded_ref, taps_ref, step // ny, step % ny).astype(BF16)
    projected = jnp.dot(latent_grad, proj_ref[...], preferred_element_type=F32)
    stage[...] = projected * column_of(share_ref[0])

    def lay(group, carry):
        for u in range(16):
            cell = group * 16 + u
            row = stage[pl.ds(cell, 1), :]
            for k in range(depth):
                slots[pl.ds(slot_ref[k * strips + step, cell], 1), :] = row
        return carry

    lax.fori_loop(0, cells // 16, lay, 0)

    @pl.when(step == strips - 1)
    def _():
        left = left_lanes(256)

        def pack(block, carry):
            at = pl.multiple_of(block * 256, 256)
            both = jnp.where(left, slots[pl.ds(at, 256), :], slots[pl.ds(half + at, 256), :])
            out_ref[pl.ds(at, 256), :] = both.astype(BF16)
            return carry

        lax.fori_loop(0, half // 256, pack, 0)


def spread(slot, padded, taps, proj, share, half):
    nx, ny, cells = padded.shape[0] - 2, padded.shape[1] - 2, padded.shape[2]
    return pl.pallas_call(
        functools.partial(spread_kernel, ny),
        grid=(nx * ny,),
        out_shape=jax.ShapeDtypeStruct((half, LANES), BF16),
        in_specs=[
            whole(pltpu.SMEM),
            whole(),
            whole(),
            whole(),
            pl.BlockSpec((1, 1, cells), lambda s: (s, 0, 0)),
        ],
        out_specs=whole(),
        scratch_shapes=[
            pltpu.VMEM((2 * half + 8, LANES), F32),
            pltpu.VMEM((cells, LANES), F32),
        ],
        compiler_params=params(),
        name="spread",
    )(slot, padded, taps, proj, share)


def settle_kernel(asked_ref, arrived_ref, out_ref, *scratch):
    sums, stage = scratch[:-1], scratch[-1]
    step = pl.program_id(0)
    per_step = arrived_ref.shape[0]
    points = out_ref.shape[1]

    @pl.when(step == 0)
    def _():
        def clear(block, carry):
            for total in sums:
                total[pl.ds(pl.multiple_of(block * LANES, LANES), LANES), :] = jnp.zeros(
                    (LANES, LANES), F32
                )
            return carry

        lax.fori_loop(0, (SPARE + points) // LANES, clear, 0)

    left = left_lanes()
    right = jnp.logical_not(left)
    ways = len(sums)
    for part in range(per_step):
        source = step * per_step + part
        stage[...] = arrived_ref[part].astype(F32)

        def add(group, carry):
            for u in range(8):
                rows = [w * (LANES // ways) + group * 8 + u for w in range(ways)]
                ones = [pl.ds(asked_ref[source, row], 1) for row in rows]
                twos = [pl.ds(asked_ref[source, row + LANES], 1) for row in rows]
                values = [stage[pl.ds(row, 1), :] for row in rows]
                new_ones = [sums[w][ones[w], :] + values[w] for w in range(ways)]
                new_twos = [sums[w][twos[w], :] + values[w] for w in range(ways)]
                for w in range(ways):
                    pltpu.store(sums[w].at[ones[w], :], new_ones[w], mask=left)
                    pltpu.store(sums[w].at[twos[w], :], new_twos[w], mask=right)
            return carry

        lax.fori_loop(0, LANES // ways // 8, add, 0)

    @pl.when(step == pl.num_programs(0) - 1)
    def _():
        def finish(block, carry):
            at = pl.multiple_of(block * LANES, LANES)
            rows = pl.ds(SPARE + at, LANES)
            total = sums[0][rows, :]
            for other in sums[1:]:
                total = total + other[rows, :]
            turned = total.T
            out_ref[:, pl.ds(at, LANES)] = turned[: LANES // 2] + turned[LANES // 2 :]
            return carry

        lax.fori_loop(0, points // LANES, finish, 0, unroll=2)


def settle(asked, arrived, points):
    sources, _ = asked.shape
    per_step = 4
    return pl.pallas_call(
        settle_kernel,
        grid=(sources // per_step,),
        out_shape=jax.ShapeDtypeStruct((LANES // 2, points), F32),
        in_specs=[
            whole(pltpu.SMEM),
            pl.BlockSpec((per_step, LANES, LANES), lambda s: (s, 0, 0)),
        ],
        out_specs=whole(),
        scratch_shapes=[pltpu.VMEM((SPARE + points, LANES), F32)] * 4
        + [pltpu.VMEM((LANES, LANES), F32)],
        compiler_params=params(),
        name="settle",
    )(asked, arrived)


def twice(matrix):
    wide = jnp.concatenate([matrix, matrix], axis=1)
    return jnp.concatenate([wide, jnp.zeros_like(wide)], axis=0)


def flipped(kernel):
    return jnp.flip(kernel, (2, 3, 4)).transpose(1, 0, 2, 3, 4)


def shards(
    point_features, neighbour_rows, neighbour_owner, valid, proj, kernel_one, kernel_two, cotangent
):
    channels, points = point_features.shape
    depth, nx, ny, cells = neighbour_rows.shape
    strips = nx * ny
    size_x, size_y = lax.axis_size("gx"), lax.axis_size("gy")
    devices = size_x * size_y
    cap = depth * strips * cells // devices
    half = devices * LANES

    def swap(array):
        return lax.all_to_all(array, ("gx", "gy"), split_axis=0, concat_axis=0, tiled=True)

    flat = (depth * strips, cells)
    slot, wanted = route(
        neighbour_owner.reshape(flat), neighbour_rows.reshape(flat), valid.reshape(flat), devices, cap
    )
    asked = swap(wanted)
    used = jnp.sum(valid.reshape(depth, strips, 1, cells), axis=0)
    share = 1.0 / jnp.maximum(used, 1).astype(F32)

    got = swap(serve(asked, point_features))

    upward = cotangent.transpose(1, 2, 3, 0)
    upward = exchange(jnp.concatenate([upward, upward], axis=-1), size_x, size_y)
    upstream = upstream_of(upward, taps_of(flipped(kernel_two)))

    latent = collect(slot, got.reshape(half, LANES), share, twice(proj))
    latent = exchange(latent.reshape(nx, ny, cells, LANES), size_x, size_y)
    gated_grad = gated(latent, taps_of(kernel_one), upstream)
    gated_grad = exchange(gated_grad.reshape(nx, ny, cells, LANES), size_x, size_y)
    outgoing = spread(slot, gated_grad, taps_of(flipped(kernel_one)), twice(proj.T), share, half)
    arrived = swap(outgoing.reshape(devices, LANES, LANES))
    return settle(asked, arrived, points)


def solution(mesh):
    placed = (
        P(None, ("gx", "gy")),
        P(None, "gx", "gy", None),
        P(None, "gx", "gy", None),
        P(None, "gx", "gy", None),
        P(),
        P(),
        P(),
        P(None, "gx", "gy", None),
    )
    return jax.shard_map(
        shards, mesh=mesh, in_specs=placed, out_specs=P(None, ("gx", "gy")), check_vma=False
    )
```

```python
import functools

import jax
import jax.numpy as jnp
from jax import lax
from jax.experimental import pallas as pl
from jax.experimental.pallas import tpu as pltpu
from jax.sharding import PartitionSpec as P

MESH = pl.DeviceIdType.MESH
SCALE_ROOT = 0.7978845608
CUBIC_TERM = 0.044715
LANES = 128
SPARE = 128
F32, BF16, I32 = jnp.float32, jnp.bfloat16, jnp.int32


def whole(space=pltpu.VMEM):
    return pl.BlockSpec(memory_space=space)


def params(mebibytes=60, **more):
    return pltpu.CompilerParams(vmem_limit_bytes=mebibytes * 1024 * 1024, **more)


def left_lanes(rows=1):
    return lax.broadcasted_iota(I32, (rows, LANES), 1) < LANES // 2


def route_kernel(owner_ref, rows_ref, valid_ref, slot_ref, want_ref, sums):
    blocks, width = owner_ref.shape
    owners, cap = want_ref.shape
    trash = owners * cap
    together = 4
    owner_of = lax.broadcasted_iota(I32, (owners, width), 0).astype(F32).astype(BF16)
    rank_of = lax.broadcasted_iota(I32, (cap, width), 0).astype(F32).astype(BF16)
    first = lax.broadcasted_iota(I32, (width, 2 * width), 0)
    second = lax.broadcasted_iota(I32, (width, 2 * width), 1)
    earlier = jnp.where((second >= width) | (first < second), 1.0, 0.0).astype(BF16)
    one, zero = jnp.ones((), BF16), jnp.zeros((), BF16)
    sums[...] = jnp.zeros_like(sums)

    def body(group, offset):
        pieces, at_rank = [], []
        for part in range(together):
            block = group * together + part
            owner = owner_ref[pl.ds(block, 1), :]
            rows = rows_ref[pl.ds(block, 1), :]
            used = valid_ref[pl.ds(block, 1), :] > 0
            hit = owner_of == jnp.where(used, owner, -1).astype(F32).astype(BF16)
            chosen = jnp.where(hit, one, zero)
            counts = jnp.dot(chosen, earlier, preferred_element_type=F32)
            before = (counts[:, :width] + offset).astype(BF16)
            offset = offset + counts[:, width:]
            rank = jnp.sum(jnp.where(hit, before, zero).astype(F32), axis=0, keepdims=True)
            at_rank.append(jnp.where(rank_of == rank.astype(BF16), one, zero))
            rank = rank.astype(I32)
            place = (rank >> 7) * (owners * LANES) + owner * LANES + (rank & 127)
            slot_ref[pl.ds(block, 1), :] = jnp.where(used, place, trash)
            high = ((rows >> 7) + 1).astype(F32).astype(BF16)
            low = (rows & 127).astype(F32).astype(BF16)
            pieces.append(
                jnp.concatenate([jnp.where(hit, high, zero), jnp.where(hit, low, zero)], axis=0)
            )
        sums[...] += lax.dot_general(
            jnp.concatenate(pieces, axis=1),
            jnp.concatenate(at_rank, axis=1),
            (((1,), (1,)), ((), ())),
            preferred_element_type=F32,
        )
        return offset

    lax.fori_loop(0, blocks // together, body, jnp.zeros((owners, width), F32))
    want_ref[...] = (sums[:owners, :] * 128.0 + sums[owners:, :]).astype(I32)


def route(owner, rows, valid, owners, cap):
    blocks, width = owner.shape
    return pl.pallas_call(
        route_kernel,
        out_shape=(
            jax.ShapeDtypeStruct((blocks, width), I32),
            jax.ShapeDtypeStruct((owners, cap), I32),
        ),
        in_specs=[whole()] * 3,
        out_specs=(whole(), whole()),
        scratch_shapes=[pltpu.VMEM((2 * owners, cap), F32)],
        compiler_params=params(),
        name="route",
    )(owner, rows, valid)


def serve_kernel(asked_ref, features_ref, out_ref, table, stage):
    step = pl.program_id(0)
    per_step = out_ref.shape[0]
    points = features_ref.shape[1]

    @pl.when(step == 0)
    def _():
        table[:SPARE, :] = jnp.zeros((SPARE, LANES), F32)

        def fill(block, carry):
            at = pl.multiple_of(block * LANES, LANES)
            part = features_ref[:, pl.ds(at, LANES)]
            table[pl.ds(SPARE + at, LANES), :] = jnp.concatenate([part, part], axis=0).T
            return carry

        lax.fori_loop(0, points // LANES, fill, 0, unroll=2)

    left = left_lanes()

    def gather(part, carry):
        asked = asked_ref.at[pl.ds((step * per_step + part) * 2 * LANES, 2 * LANES)]
        for row in range(LANES):
            one = table[pl.ds(asked[row], 1), :]
            two = table[pl.ds(asked[row + LANES], 1), :]
            stage[row : row + 1, :] = jnp.where(left, one, two)
        out_ref[part] = stage[...].astype(BF16)
        return carry

    lax.fori_loop(0, per_step, gather, 0)


def serve(asked, features):
    sources = asked.shape[0] // (2 * LANES)
    points = features.shape[1]
    per_step = 4
    return pl.pallas_call(
        serve_kernel,
        grid=(sources // per_step,),
        out_shape=jax.ShapeDtypeStruct((sources, LANES, LANES), BF16),
        in_specs=[whole(pltpu.SMEM), whole()],
        out_specs=pl.BlockSpec((per_step, LANES, LANES), lambda s: (s, 0, 0)),
        scratch_shapes=[
            pltpu.VMEM((SPARE + points, LANES), F32),
            pltpu.VMEM((LANES, LANES), F32),
        ],
        compiler_params=params(),
        name="serve",
    )(asked, features)


def column_of(row):
    return jnp.broadcast_to(row, (LANES, row.shape[1])).T


def collect_kernel(slot_ref, got_ref, share_ref, proj_ref, out_ref, table, stage):
    step = pl.program_id(0)
    strips = pl.num_programs(0)
    half = got_ref.shape[0]
    cells = stage.shape[0]
    depth = slot_ref.shape[0] // strips // cells

    @pl.when(step == 0)
    def _():
        left = left_lanes(256)

        def fill(block, carry):
            at = pl.multiple_of(block * 256, 256)
            part = got_ref[pl.ds(at, 256), :].astype(F32)
            table[pl.ds(at, 256), :] = jnp.where(left, part, 0.0)
            table[pl.ds(half + at, 256), :] = jnp.where(left, 0.0, part)
            return carry

        lax.fori_loop(0, half // 256, fill, 0)
        table[2 * half :, :] = jnp.zeros((8, LANES), F32)

    place = [slot_ref.at[pl.ds((k * strips + step) * cells, cells)] for k in range(depth)]
    for cell in range(cells):
        rows = [table[pl.ds(place[k][cell], 1), :] for k in range(depth)]
        stage[cell : cell + 1, :] = (rows[0] + rows[1]) + (rows[2] + rows[3])
    total = stage[...]
    total = total + pltpu.roll(total, LANES // 2, 1)
    averaged = (total * column_of(share_ref[0])).astype(BF16)
    out_ref[0] = jnp.dot(averaged, proj_ref[...], preferred_element_type=F32).astype(BF16)


def collect(slot, got, share, proj):
    strips, _, cells = share.shape
    half = got.shape[0]
    return pl.pallas_call(
        collect_kernel,
        grid=(strips,),
        out_shape=jax.ShapeDtypeStruct((strips, cells, LANES), BF16),
        in_specs=[
            whole(pltpu.SMEM),
            whole(),
            pl.BlockSpec((1, 1, cells), lambda s: (s, 0, 0)),
            whole(),
        ],
        out_specs=pl.BlockSpec((1, cells, LANES), lambda s: (s, 0, 0)),
        scratch_shapes=[
            pltpu.VMEM((2 * half + 8, LANES), F32),
            pltpu.VMEM((cells, LANES), F32),
        ],
        compiler_params=params(),
        name="collect",
    )(slot, got, share, proj)


AROUND = ((1, 0), (-1, 0), (0, 1), (0, -1), (1, 1), (1, -1), (-1, 1), (-1, -1))


def exchange_kernel(
    size_x, size_y, rows_ref, out_ref, send_x, send_y, come_x, come_y, come_c, sent, come
):
    i, j = lax.axis_index("gx"), lax.axis_index("gy")
    nx, ny, cells, _ = rows_ref.shape
    left = left_lanes(cells)

    def device(di, dj):
        return (lax.rem(i + di + size_x, size_x), lax.rem(j + dj + size_y, size_y))

    barrier = pltpu.get_barrier_semaphore()
    for di, dj in AROUND:
        pl.semaphore_signal(barrier, inc=1, device_id=device(di, dj), device_id_type=MESH)
    pl.semaphore_wait(barrier, len(AROUND))

    for at, x in ((0, nx - 1), (1, 0)):
        for q in range(ny // 2):
            send_x[at, q] = jnp.where(left, rows_ref[x, 2 * q], rows_ref[x, 2 * q + 1])
    for at, y in ((0, ny - 1), (1, 0)):
        for q in range(nx // 2):
            send_y[at, q] = jnp.where(left, rows_ref[2 * q, y], rows_ref[2 * q + 1, y])
    copies = []
    for at, (di, dj) in enumerate(AROUND):
        if dj == 0:
            pair = (send_x.at[at], come_x.at[at])
        elif di == 0:
            pair = (send_y.at[at - 2], come_y.at[at - 2])
        else:
            pair = (
                rows_ref.at[nx - 1 if di > 0 else 0, ny - 1 if dj > 0 else 0],
                come_c.at[at - 4],
            )
        copies.append(
            pltpu.make_async_remote_copy(
                src_ref=pair[0],
                dst_ref=pair[1],
                send_sem=sent.at[at],
                recv_sem=come.at[at],
                device_id=device(di, dj),
                device_id_type=MESH,
            )
        )
        copies[-1].start()
    for x in range(nx):
        for y in range(ny):
            out_ref[x + 1, y + 1] = rows_ref[x, y]
    for copy in copies:
        copy.wait()

    def apart(ref, at, q):
        both = ref[at, q].astype(F32)
        turned = pltpu.roll(both, LANES // 2, 1)
        return jnp.where(left, both, turned), jnp.where(left, turned, both)

    inside_x = (i > 0, i < size_x - 1)
    inside_y = (j > 0, j < size_y - 1)
    for at, x in ((0, 0), (1, nx + 1)):
        for q in range(ny // 2):
            for p, row in enumerate(apart(come_x, at, q)):
                out_ref[x, 2 * q + p + 1] = jnp.where(inside_x[at], row, 0.0).astype(BF16)
    for at, y in ((0, 0), (1, ny + 1)):
        for q in range(nx // 2):
            for p, row in enumerate(apart(come_y, at, q)):
                out_ref[2 * q + p + 1, y] = jnp.where(inside_y[at], row, 0.0).astype(BF16)
    for at, (di, dj) in enumerate(AROUND[4:]):
        ax, ay = (0 if di > 0 else 1), (0 if dj > 0 else 1)
        keep = inside_x[ax] & inside_y[ay]
        row = jnp.where(keep, come_c[at].astype(F32), 0.0).astype(BF16)
        out_ref[0 if di > 0 else nx + 1, 0 if dj > 0 else ny + 1] = row


def exchange(rows, size_x, size_y):
    nx, ny, cells, _ = rows.shape
    return pl.pallas_call(
        functools.partial(exchange_kernel, size_x, size_y),
        out_shape=jax.ShapeDtypeStruct((nx + 2, ny + 2, cells, LANES), BF16),
        in_specs=[whole()],
        out_specs=whole(),
        scratch_shapes=[
            pltpu.VMEM((2, ny // 2, cells, LANES), BF16),
            pltpu.VMEM((2, nx // 2, cells, LANES), BF16),
            pltpu.VMEM((2, ny // 2, cells, LANES), BF16),
            pltpu.VMEM((2, nx // 2, cells, LANES), BF16),
            pltpu.VMEM((4, cells, LANES), BF16),
            pltpu.SemaphoreType.DMA((8,)),
            pltpu.SemaphoreType.DMA((8,)),
        ],
        compiler_params=params(collective_id=0, has_side_effects=True),
        name="exchange",
    )(rows)


def gelu_slope(value):
    inner = SCALE_ROOT * (value + CUBIC_TERM * value * value * value)
    tangent = jnp.tanh(inner)
    return 0.5 * (1.0 + tangent) + 0.5 * value * (1.0 - tangent * tangent) * SCALE_ROOT * (
        1.0 + 3.0 * CUBIC_TERM * value * value
    )


def taps_of(kernel):
    o, i = kernel.shape[:2]
    taps = kernel.transpose(2, 3, 1, 4, 0)
    taps = jnp.concatenate([taps, jnp.zeros((3, 1, i, 3, o), taps.dtype)], axis=1)
    return jnp.concatenate([taps, taps], axis=-1).reshape(12 * i, 6 * o)


def conv_strip(padded_ref, taps_ref, x, y):
    cells = padded_ref.shape[2]
    left = left_lanes(cells)
    parts = []
    for a in range(3):
        parts.append(jnp.where(left, padded_ref[x + a, y], padded_ref[x + a, y + 1]))
        parts.append(padded_ref[x + a, y + 2])
    sums = jnp.dot(jnp.concatenate(parts, axis=1), taps_ref[...], preferred_element_type=F32)
    depth = lax.broadcasted_iota(I32, (cells, LANES), 0)
    low = jnp.where(depth == 0, 0.0, pltpu.roll(sums[:, :LANES], 1, 0))
    high = jnp.where(depth == cells - 1, 0.0, pltpu.roll(sums[:, 2 * LANES :], cells - 1, 0))
    return sums[:, LANES : 2 * LANES] + low + high


def upstream_kernel(ny, padded_ref, taps_ref, out_ref):
    step = pl.program_id(0)
    out_ref[0] = conv_strip(padded_ref, taps_ref, step // ny, step % ny)


def gate_kernel(ny, padded_ref, taps_ref, upstream_ref, out_ref):
    step = pl.program_id(0)
    preact = conv_strip(padded_ref, taps_ref, step // ny, step % ny)
    out_ref[0] = (upstream_ref[0] * gelu_slope(preact)).astype(BF16)


def strip_spec(cells):
    return pl.BlockSpec((1, cells, LANES), lambda s: (s, 0, 0))


def conv_cost(strips, cells):
    return pl.CostEstimate(
        flops=2 * strips * cells * 12 * 64 * 6 * 64, bytes_accessed=12 << 20, transcendentals=0
    )


def upstream_of(padded, taps):
    nx, ny, cells = padded.shape[0] - 2, padded.shape[1] - 2, padded.shape[2]
    return pl.pallas_call(
        functools.partial(upstream_kernel, ny),
        grid=(nx * ny,),
        out_shape=jax.ShapeDtypeStruct((nx * ny, cells, LANES), F32),
        in_specs=[whole(), whole()],
        out_specs=strip_spec(cells),
        compiler_params=params(),
        cost_estimate=conv_cost(nx * ny, cells),
        name="upstream",
    )(padded, taps)


def gated(padded, taps, upstream):
    nx, ny, cells = padded.shape[0] - 2, padded.shape[1] - 2, padded.shape[2]
    return pl.pallas_call(
        functools.partial(gate_kernel, ny),
        grid=(nx * ny,),
        out_shape=jax.ShapeDtypeStruct((nx * ny, cells, LANES), BF16),
        in_specs=[whole(), whole(), strip_spec(cells)],
        out_specs=strip_spec(cells),
        compiler_params=params(),
        cost_estimate=conv_cost(nx * ny, cells),
        name="gated",
    )(padded, taps, upstream)


def spread_kernel(ny, slot_ref, padded_ref, taps_ref, proj_ref, share_ref, out_ref, slots, stage):
    step = pl.program_id(0)
    strips = pl.num_programs(0)
    half = out_ref.shape[0]
    cells = stage.shape[0]
    depth = slot_ref.shape[0] // strips // cells

    @pl.when(step == 0)
    def _():
        def clear(block, carry):
            slots[pl.ds(pl.multiple_of(block * 256, 256), 256), :] = jnp.zeros((256, LANES), F32)
            return carry

        lax.fori_loop(0, 2 * half // 256, clear, 0)

    latent_grad = conv_strip(padded_ref, taps_ref, step // ny, step % ny).astype(BF16)
    projected = jnp.dot(latent_grad, proj_ref[...], preferred_element_type=F32)
    stage[...] = projected * column_of(share_ref[0])

    place = [slot_ref.at[pl.ds((k * strips + step) * cells, cells)] for k in range(depth)]
    for cell in range(cells):
        row = stage[cell : cell + 1, :]
        for k in range(depth):
            slots[pl.ds(place[k][cell], 1), :] = row

    @pl.when(step == strips - 1)
    def _():
        left = left_lanes(256)

        def pack(block, carry):
            at = pl.multiple_of(block * 256, 256)
            both = jnp.where(left, slots[pl.ds(at, 256), :], slots[pl.ds(half + at, 256), :])
            out_ref[pl.ds(at, 256), :] = both.astype(BF16)
            return carry

        lax.fori_loop(0, half // 256, pack, 0)


def spread(slot, padded, taps, proj, share, half):
    nx, ny, cells = padded.shape[0] - 2, padded.shape[1] - 2, padded.shape[2]
    return pl.pallas_call(
        functools.partial(spread_kernel, ny),
        grid=(nx * ny,),
        out_shape=jax.ShapeDtypeStruct((half, LANES), BF16),
        in_specs=[
            whole(pltpu.SMEM),
            whole(),
            whole(),
            whole(),
            pl.BlockSpec((1, 1, cells), lambda s: (s, 0, 0)),
        ],
        out_specs=whole(),
        scratch_shapes=[
            pltpu.VMEM((2 * half + 8, LANES), F32),
            pltpu.VMEM((cells, LANES), F32),
        ],
        compiler_params=params(),
        name="spread",
    )(slot, padded, taps, proj, share)


def settle_kernel(asked_ref, arrived_ref, out_ref, *scratch):
    sums, stage = scratch[:-1], scratch[-1]
    step = pl.program_id(0)
    per_step = arrived_ref.shape[0]
    points = out_ref.shape[1]

    @pl.when(step == 0)
    def _():
        def clear(block, carry):
            for total in sums:
                total[pl.ds(pl.multiple_of(block * LANES, LANES), LANES), :] = jnp.zeros(
                    (LANES, LANES), F32
                )
            return carry

        lax.fori_loop(0, (SPARE + points) // LANES, clear, 0)

    left = left_lanes()
    right = jnp.logical_not(left)
    ways = len(sums)
    def add(part, carry):
        asked = asked_ref.at[pl.ds((step * per_step + part) * 2 * LANES, 2 * LANES)]
        stage[...] = arrived_ref[part].astype(F32)
        for row in range(LANES // ways):
            rows = [w * (LANES // ways) + row for w in range(ways)]
            ones = [pl.ds(asked[row], 1) for row in rows]
            twos = [pl.ds(asked[row + LANES], 1) for row in rows]
            values = [stage[row : row + 1, :] for row in rows]
            new_ones = [sums[w][ones[w], :] + values[w] for w in range(ways)]
            new_twos = [sums[w][twos[w], :] + values[w] for w in range(ways)]
            for w in range(ways):
                pltpu.store(sums[w].at[ones[w], :], new_ones[w], mask=left)
                pltpu.store(sums[w].at[twos[w], :], new_twos[w], mask=right)
        return carry

    lax.fori_loop(0, per_step, add, 0)

    @pl.when(step == pl.num_programs(0) - 1)
    def _():
        def finish(block, carry):
            at = pl.multiple_of(block * LANES, LANES)
            rows = pl.ds(SPARE + at, LANES)
            total = sums[0][rows, :]
            for other in sums[1:]:
                total = total + other[rows, :]
            turned = total.T
            out_ref[:, pl.ds(at, LANES)] = turned[: LANES // 2] + turned[LANES // 2 :]
            return carry

        lax.fori_loop(0, points // LANES, finish, 0, unroll=2)


def settle(asked, arrived, points):
    sources = arrived.shape[0]
    per_step = 4
    return pl.pallas_call(
        settle_kernel,
        grid=(sources // per_step,),
        out_shape=jax.ShapeDtypeStruct((LANES // 2, points), F32),
        in_specs=[
            whole(pltpu.SMEM),
            pl.BlockSpec((per_step, LANES, LANES), lambda s: (s, 0, 0)),
        ],
        out_specs=whole(),
        scratch_shapes=[pltpu.VMEM((SPARE + points, LANES), F32)] * 4
        + [pltpu.VMEM((LANES, LANES), F32)],
        compiler_params=params(),
        name="settle",
    )(asked, arrived)


def twice(matrix):
    wide = jnp.concatenate([matrix, matrix], axis=1)
    return jnp.concatenate([wide, jnp.zeros_like(wide)], axis=0)


def flipped(kernel):
    return jnp.flip(kernel, (2, 3, 4)).transpose(1, 0, 2, 3, 4)


def shards(
    point_features, neighbour_rows, neighbour_owner, valid, proj, kernel_one, kernel_two, cotangent
):
    channels, points = point_features.shape
    depth, nx, ny, cells = neighbour_rows.shape
    strips = nx * ny
    size_x, size_y = lax.axis_size("gx"), lax.axis_size("gy")
    devices = size_x * size_y
    cap = depth * strips * cells // devices
    half = devices * LANES

    def swap(array):
        return lax.all_to_all(array, ("gx", "gy"), split_axis=0, concat_axis=0, tiled=True)

    flat = (depth * strips, cells)
    slot, wanted = route(
        neighbour_owner.reshape(flat), neighbour_rows.reshape(flat), valid.reshape(flat), devices, cap
    )
    asked = swap(wanted).reshape(-1)
    slot = slot.reshape(-1)
    used = jnp.sum(valid.reshape(depth, strips, 1, cells), axis=0)
    share = 1.0 / jnp.maximum(used, 1).astype(F32)

    got = swap(serve(asked, point_features))

    upward = cotangent.transpose(1, 2, 3, 0)
    upward = exchange(jnp.concatenate([upward, upward], axis=-1), size_x, size_y)
    upstream = upstream_of(upward, taps_of(flipped(kernel_two)))

    latent = collect(slot, got.reshape(half, LANES), share, twice(proj))
    latent = exchange(latent.reshape(nx, ny, cells, LANES), size_x, size_y)
    gated_grad = gated(latent, taps_of(kernel_one), upstream)
    gated_grad = exchange(gated_grad.reshape(nx, ny, cells, LANES), size_x, size_y)
    outgoing = spread(slot, gated_grad, taps_of(flipped(kernel_one)), twice(proj.T), share, half)
    arrived = swap(outgoing.reshape(devices, LANES, LANES))
    return settle(asked, arrived, points)


def solution(mesh):
    placed = (
        P(None, ("gx", "gy")),
        P(None, "gx", "gy", None),
        P(None, "gx", "gy", None),
        P(None, "gx", "gy", None),
        P(),
        P(),
        P(),
        P(None, "gx", "gy", None),
    )
    return jax.shard_map(
        shards, mesh=mesh, in_specs=placed, out_specs=P(None, ("gx", "gy")), check_vma=False
    )
```

```python
import functools

import jax
import jax.numpy as jnp
from jax import lax
from jax.experimental import pallas as pl
from jax.experimental.pallas import tpu as pltpu
from jax.sharding import PartitionSpec as P

MESH = pl.DeviceIdType.MESH
SCALE_ROOT = 0.7978845608
CUBIC_TERM = 0.044715
LANES = 128
SPARE = 128
F32, BF16, I32 = jnp.float32, jnp.bfloat16, jnp.int32


def whole(space=pltpu.VMEM):
    return pl.BlockSpec(memory_space=space)


def params(mebibytes=60, **more):
    return pltpu.CompilerParams(vmem_limit_bytes=mebibytes * 1024 * 1024, **more)


def left_lanes(rows=1):
    return lax.broadcasted_iota(I32, (rows, LANES), 1) < LANES // 2


CHUNK = 1024


def chunks_of(list_ref, held, sems, step, work, order=lambda step: step):
    def copy(which, step):
        start = pl.multiple_of((2 * order(step) + which) * CHUNK, CHUNK)
        return pltpu.make_async_copy(list_ref.at[pl.ds(start, CHUNK)], held[which], sems.at[which])

    @pl.when(step == 0)
    def _():
        for which in range(2):
            copy(which, 0).start()

    for which in range(2):
        copy(which, step).wait()
        work(which, held[which])

        @pl.when(step < pl.num_programs(0) - 1)
        def _():
            copy(which, step + 1).start()


LISTS = [pltpu.SMEM((CHUNK,), I32), pltpu.SMEM((CHUNK,), I32), pltpu.SemaphoreType.DMA((2,))]


def route_kernel(strips, owner_ref, rows_ref, valid_ref, slot_ref, want_ref, sums):
    blocks, width = owner_ref.shape
    owners, cap = want_ref.shape
    trash = owners * cap
    together = 4
    owner_of = lax.broadcasted_iota(I32, (owners, width), 0).astype(F32).astype(BF16)
    rank_of = lax.broadcasted_iota(I32, (cap, width), 0).astype(F32).astype(BF16)
    first = lax.broadcasted_iota(I32, (width, 2 * width), 0)
    second = lax.broadcasted_iota(I32, (width, 2 * width), 1)
    earlier = jnp.where((second >= width) | (first < second), 1.0, 0.0).astype(BF16)
    one, zero = jnp.ones((), BF16), jnp.zeros((), BF16)
    sums[...] = jnp.zeros_like(sums)

    def body(group, offset):
        pieces, at_rank = [], []
        for part in range(together):
            block = group * together + part
            owner = owner_ref[pl.ds(block, 1), :]
            rows = rows_ref[pl.ds(block, 1), :]
            used = valid_ref[pl.ds(block, 1), :] > 0
            hit = owner_of == jnp.where(used, owner, -1).astype(F32).astype(BF16)
            chosen = jnp.where(hit, one, zero)
            counts = jnp.dot(chosen, earlier, preferred_element_type=F32)
            before = (counts[:, :width] + offset).astype(BF16)
            offset = offset + counts[:, width:]
            rank = jnp.sum(jnp.where(hit, before, zero).astype(F32), axis=0, keepdims=True)
            at_rank.append(jnp.where(rank_of == rank.astype(BF16), one, zero))
            rank = rank.astype(I32)
            place = (rank >> 7) * (owners * LANES) + owner * LANES + (rank & 127)
            at = block % strips * (blocks // strips) + block // strips
            slot_ref[pl.ds(at, 1), :] = jnp.where(used, place, trash)
            high = ((rows >> 7) + 1).astype(F32).astype(BF16)
            low = (rows & 127).astype(F32).astype(BF16)
            pieces.append(
                jnp.concatenate([jnp.where(hit, high, zero), jnp.where(hit, low, zero)], axis=0)
            )
        sums[...] += lax.dot_general(
            jnp.concatenate(pieces, axis=1),
            jnp.concatenate(at_rank, axis=1),
            (((1,), (1,)), ((), ())),
            preferred_element_type=F32,
        )
        return offset

    lax.fori_loop(0, blocks // together, body, jnp.zeros((owners, width), F32))
    want_ref[...] = (sums[:owners, :] * 128.0 + sums[owners:, :]).astype(I32)


def route(owner, rows, valid, strips, owners, cap):
    blocks, width = owner.shape
    return pl.pallas_call(
        functools.partial(route_kernel, strips),
        out_shape=(
            jax.ShapeDtypeStruct((blocks, width), I32),
            jax.ShapeDtypeStruct((owners, cap), I32),
        ),
        in_specs=[whole()] * 3,
        out_specs=(whole(), whole()),
        scratch_shapes=[pltpu.VMEM((2 * owners, cap), F32)],
        compiler_params=params(),
        name="route",
    )(owner, rows, valid)


def table_kernel(features_ref, out_ref):
    points = features_ref.shape[1]
    out_ref[:SPARE, :] = jnp.zeros((SPARE, LANES), F32)

    def fill(block, carry):
        at = pl.multiple_of(block * LANES, LANES)
        part = features_ref[:, pl.ds(at, LANES)]
        out_ref[pl.ds(SPARE + at, LANES), :] = jnp.concatenate([part, part], axis=0).T
        return carry

    lax.fori_loop(0, points // LANES, fill, 0, unroll=4)


def table_of(features):
    channels, points = features.shape
    return pl.pallas_call(
        table_kernel,
        out_shape=jax.ShapeDtypeStruct((SPARE + points, LANES), F32),
        in_specs=[whole()],
        out_specs=whole(),
        compiler_params=params(),
        cost_estimate=pl.CostEstimate(flops=0, bytes_accessed=32 << 20, transcendentals=0),
        name="table",
    )(features)


def serve_kernel(asked_ref, table, out_ref, stage, one_list, other_list, sems):
    step = pl.program_id(0)
    held = (one_list, other_list)
    per_step = out_ref.shape[0]

    left = left_lanes()

    def gather(which, asked):
        for part in range(CHUNK // (2 * LANES)):
            at = part * 2 * LANES
            for row in range(LANES):
                one = table[pl.ds(asked[at + row], 1), :]
                two = table[pl.ds(asked[at + row + LANES], 1), :]
                stage[part, row : row + 1, :] = jnp.where(left, one, two)
            out_ref[which * (per_step // 2) + part] = stage[part].astype(BF16)

    chunks_of(asked_ref, held, sems, step, gather)


def serve(asked, table):
    sources = asked.shape[0] // (2 * LANES)
    per_step = 2 * CHUNK // (2 * LANES)
    return pl.pallas_call(
        serve_kernel,
        grid=(sources // per_step,),
        out_shape=jax.ShapeDtypeStruct((sources, LANES, LANES), BF16),
        in_specs=[whole(pl.ANY), whole()],
        out_specs=pl.BlockSpec((per_step, LANES, LANES), lambda s: (s, 0, 0)),
        scratch_shapes=[
            pltpu.VMEM((per_step // 2, LANES, LANES), F32),
            *LISTS,
        ],
        compiler_params=params(),
        name="serve",
    )(asked, table)


AROUND = ((1, 0), (-1, 0), (1, 1), (1, -1), (-1, 1), (-1, -1), (0, 1), (0, -1))
X_SENDS, Y_SENDS = range(6), range(6, 8)


def rim_first(nx, ny, step):
    pairs = ny // 2
    late = step // (2 * pairs)
    at = step - 2 * pairs
    inner = nx - 2
    ends = at // (2 * inner)
    first = (step // pairs) * (nx - 1) * pairs + step % pairs
    end = (1 + at // 2) * pairs + (at % 2) * (pairs - 1)
    rest = at - 2 * inner
    middle = (1 + rest // (pairs - 2)) * pairs + 1 + rest % (pairs - 2)
    return (1 - late) * first + late * ((1 - ends) * end + ends * middle)


def rim_steps(nx, ny):
    return ny - 1, ny - 1 + 2 * (nx - 2)


class Rims:
    def __init__(self, sizes, out_ref, send_x, send_y, send_c, come_x, come_y, come_c, sent, come):
        self.sizes, self.out = sizes, out_ref
        self.at = (lax.axis_index("gx"), lax.axis_index("gy"))
        self.nx, self.ny = out_ref.shape[0] - 2, out_ref.shape[1] - 2
        self.cells = out_ref.shape[2]
        self.send, self.come = (send_x, send_y, send_c), (come_x, come_y, come_c)
        self.sems = (sent, come)

    def device(self, di, dj):
        (i, j), (size_x, size_y) = self.at, self.sizes
        return (lax.rem(i + di + size_x, size_x), lax.rem(j + dj + size_y, size_y))

    def copy(self, number):
        kind, at = (0, number) if number < 2 else (2, number - 2) if number < 6 else (1, number - 6)
        return pltpu.make_async_remote_copy(
            src_ref=self.send[kind].at[at],
            dst_ref=self.come[kind].at[at],
            send_sem=self.sems[0].at[number],
            recv_sem=self.sems[1].at[number],
            device_id=self.device(*AROUND[number]),
            device_id_type=MESH,
        )

    def greet(self):
        barrier = pltpu.get_barrier_semaphore()
        for di, dj in AROUND:
            pl.semaphore_signal(barrier, inc=1, device_id=self.device(di, dj), device_id_type=MESH)

    def send_first(self):
        pl.semaphore_wait(pltpu.get_barrier_semaphore(), len(AROUND))
        left = left_lanes(self.cells)
        deep = self.cells // 2
        for number in X_SENDS:
            di, dj = AROUND[number]
            x = self.nx if di > 0 else 1
            if dj == 0:
                for q in range(self.ny // 2):
                    self.send[0][number, q] = jnp.where(
                        left, self.out[x, 2 * q + 1], self.out[x, 2 * q + 2]
                    )
            else:
                row = self.out.at[x, self.ny if dj > 0 else 1]
                self.send[2][number - 2] = jnp.where(left[:deep], row[:deep, :], row[deep:, :])
            self.copy(number).start()

    def send_last(self):
        left = left_lanes(self.cells)
        for number in Y_SENDS:
            y = self.ny if AROUND[number][1] > 0 else 1
            for q in range(self.nx // 2):
                self.send[1][number - 6, q] = jnp.where(
                    left, self.out[2 * q + 1, y], self.out[2 * q + 2, y]
                )
            self.copy(number).start()

    def finish(self):
        left = left_lanes(self.cells)
        deep = self.cells // 2
        (i, j), (size_x, size_y) = self.at, self.sizes
        come_x, come_y, come_c = self.come

        def apart(both, keep):
            both = jnp.where(keep, both.astype(F32), 0.0)
            turned = pltpu.roll(both, LANES // 2, 1)
            side = left[: both.shape[0]]
            return (
                jnp.where(side, both, turned).astype(BF16),
                jnp.where(side, turned, both).astype(BF16),
            )

        for number, (di, dj) in enumerate(AROUND):
            self.copy(number).wait()
            keep_x = (i > 0) if di > 0 else (i < size_x - 1)
            keep_y = (j > 0) if dj > 0 else (j < size_y - 1)
            x = 0 if di > 0 else self.nx + 1
            y = 0 if dj > 0 else self.ny + 1
            if dj == 0:
                for q in range(self.ny // 2):
                    for p, row in enumerate(apart(come_x[number, q], keep_x)):
                        self.out[x, 2 * q + p + 1] = row
            elif di == 0:
                for q in range(self.nx // 2):
                    for p, row in enumerate(apart(come_y[number - 6, q], keep_y)):
                        self.out[2 * q + p + 1, y] = row
            else:
                place = self.out.at[x, y]
                for p, row in enumerate(apart(come_c[number - 2], keep_x & keep_y)):
                    place[p * deep : (p + 1) * deep, :] = row

    def around(self, step, work):
        first, last = rim_steps(self.nx, self.ny)

        @pl.when(step == 0)
        def _():
            self.greet()

        work()

        @pl.when(step == first)
        def _():
            self.send_first()

        @pl.when(step == last)
        def _():
            self.send_last()

        @pl.when(step == pl.num_programs(0) - 1)
        def _():
            self.finish()


def rim_scratch(nx, ny, cells):
    def buffers():
        return [
            pltpu.VMEM((2, ny // 2, cells, LANES), BF16),
            pltpu.VMEM((2, nx // 2, cells, LANES), BF16),
            pltpu.VMEM((4, cells // 2, LANES), BF16),
        ]

    return [*buffers(), *buffers(), pltpu.SemaphoreType.DMA((8,)), pltpu.SemaphoreType.DMA((8,))]


def column_of(row):
    return jnp.broadcast_to(row, (LANES, row.shape[1])).T


def collect_kernel(
    sizes,
    slot_ref,
    got_ref,
    share_ref,
    proj_ref,
    out_ref,
    table,
    stage,
    one_list,
    other_list,
    sems,
    *rim_refs,
):
    step = pl.program_id(0)
    nx, ny = out_ref.shape[0] - 2, out_ref.shape[1] - 2
    order = functools.partial(rim_first, nx, ny)
    pair = order(step)
    x, y = pair // (ny // 2), pair % (ny // 2) * 2
    half = got_ref.shape[0]
    cells = stage.shape[1]
    depth = CHUNK // cells

    @pl.when(step == 0)
    def _():
        left = left_lanes(256)

        def fill(block, carry):
            at = pl.multiple_of(block * 256, 256)
            part = got_ref[pl.ds(at, 256), :].astype(F32)
            table[pl.ds(at, 256), :] = jnp.where(left, part, 0.0)
            table[pl.ds(half + at, 256), :] = jnp.where(left, 0.0, part)
            return carry

        lax.fori_loop(0, half // 256, fill, 0)
        table[2 * half :, :] = jnp.zeros((8, LANES), F32)

    def gather(which, slot):
        for cell in range(cells):
            total = table[pl.ds(slot[cell], 1), :]
            for k in range(1, depth):
                total = total + table[pl.ds(slot[k * cells + cell], 1), :]
            stage[which, cell : cell + 1, :] = total
        total = stage[which]
        total = total + pltpu.roll(total, LANES // 2, 1)
        averaged = (total * column_of(share_ref[which])).astype(BF16)
        latent = jnp.dot(averaged, proj_ref[...], preferred_element_type=F32).astype(BF16)
        out_ref[x + 1, y + which + 1] = latent

    def work():
        chunks_of(slot_ref, (one_list, other_list), sems, step, gather, order)

    Rims(sizes, out_ref, *rim_refs).around(step, work)


def collect(sizes, nx, ny, slot, got, share, proj):
    strips, _, cells = share.shape
    half = got.shape[0]
    return pl.pallas_call(
        functools.partial(collect_kernel, sizes),
        grid=(strips // 2,),
        out_shape=jax.ShapeDtypeStruct((nx + 2, ny + 2, cells, LANES), BF16),
        in_specs=[
            whole(pl.ANY),
            whole(),
            pl.BlockSpec((2, 1, cells), lambda s: (rim_first(nx, ny, s), 0, 0)),
            whole(),
        ],
        out_specs=whole(),
        scratch_shapes=[
            pltpu.VMEM((2 * half + 8, LANES), F32),
            pltpu.VMEM((2, cells, LANES), F32),
            *LISTS,
            *rim_scratch(nx, ny, cells),
        ],
        compiler_params=params(collective_id=0, has_side_effects=True),
        name="collect",
    )(slot, got, share, proj)


def gelu_slope(value):
    inner = SCALE_ROOT * (value + CUBIC_TERM * value * value * value)
    tangent = jnp.tanh(inner)
    return 0.5 * (1.0 + tangent) + 0.5 * value * (1.0 - tangent * tangent) * SCALE_ROOT * (
        1.0 + 3.0 * CUBIC_TERM * value * value
    )


def taps_of(kernel):
    o, i = kernel.shape[:2]
    taps = kernel.transpose(2, 3, 1, 4, 0)
    taps = jnp.concatenate([taps, jnp.zeros((3, 1, i, 3, o), taps.dtype)], axis=1)
    order = [taps[..., c, :] for c in (1, 0, 2, 1)]
    return jnp.concatenate(order, axis=-1).reshape(12 * i, 4 * o)


def conv_strips(padded_ref, taps_ref, x, y):
    cells = padded_ref.shape[2]
    left = left_lanes(cells)
    strips = []
    for q in range(2):
        parts = []
        for a in range(3):
            parts.append(jnp.where(left, padded_ref[x + a, y + q], padded_ref[x + a, y + q + 1]))
            parts.append(padded_ref[x + a, y + q + 2])
        strips.append(jnp.concatenate(parts, axis=1))
    sums = jnp.dot(jnp.concatenate(strips, axis=0), taps_ref[...], preferred_element_type=F32)
    depth = lax.broadcasted_iota(I32, (cells, LANES), 0)
    results = []
    for q in range(2):
        one = sums[q * cells : (q + 1) * cells, :LANES]
        two = sums[q * cells : (q + 1) * cells, LANES:]
        below = jnp.where(depth == 0, 0.0, pltpu.roll(one, 1, 0))
        above = jnp.where(depth == cells - 1, 0.0, pltpu.roll(two, cells - 1, 0))
        sides = jnp.where(left, above, below)
        here = jnp.where(left, one, two)
        results.append(here + sides + pltpu.roll(sides, LANES // 2, 1))
    return results


def place_of(ny):
    first = 2 * pl.program_id(0)
    return first // ny, first % ny


def upstream_kernel(ny, padded_ref, taps_ref, out_ref):
    for q, strip in enumerate(conv_strips(padded_ref, taps_ref, *place_of(ny))):
        out_ref[q] = strip


def gate_kernel(sizes, padded_ref, taps_ref, upstream_ref, out_ref, *rim_refs):
    step = pl.program_id(0)
    nx, ny = out_ref.shape[0] - 2, out_ref.shape[1] - 2
    pair = rim_first(nx, ny, step)
    x, y = pair // (ny // 2), pair % (ny // 2) * 2

    def work():
        for q, preact in enumerate(conv_strips(padded_ref, taps_ref, x, y)):
            gated_grad = (upstream_ref[q] * gelu_slope(preact)).astype(BF16)
            out_ref[x + 1, y + q + 1] = gated_grad

    Rims(sizes, out_ref, *rim_refs).around(step, work)


def strip_spec(cells):
    return pl.BlockSpec((2, cells, LANES), lambda s: (s, 0, 0))


def conv_cost(strips, cells):
    return pl.CostEstimate(
        flops=2 * strips * cells * 12 * 64 * 4 * 64, bytes_accessed=12 << 20, transcendentals=0
    )


def upstream_of(padded, taps):
    nx, ny, cells = padded.shape[0] - 2, padded.shape[1] - 2, padded.shape[2]
    return pl.pallas_call(
        functools.partial(upstream_kernel, ny),
        grid=(nx * ny // 2,),
        out_shape=jax.ShapeDtypeStruct((nx * ny, cells, LANES), F32),
        in_specs=[whole(), whole()],
        out_specs=strip_spec(cells),
        compiler_params=params(),
        cost_estimate=conv_cost(nx * ny, cells),
        name="upstream",
    )(padded, taps)


def gated(sizes, padded, taps, upstream):
    nx, ny, cells = padded.shape[0] - 2, padded.shape[1] - 2, padded.shape[2]
    return pl.pallas_call(
        functools.partial(gate_kernel, sizes),
        grid=(nx * ny // 2,),
        out_shape=jax.ShapeDtypeStruct(padded.shape, BF16),
        in_specs=[
            whole(),
            whole(),
            pl.BlockSpec((2, cells, LANES), lambda s: (rim_first(nx, ny, s), 0, 0)),
        ],
        out_specs=whole(),
        scratch_shapes=rim_scratch(nx, ny, cells),
        compiler_params=params(collective_id=1, has_side_effects=True),
        cost_estimate=conv_cost(nx * ny, cells),
        name="gated",
    )(padded, taps, upstream)


def spread_kernel(
    ny,
    slot_ref,
    padded_ref,
    taps_ref,
    proj_ref,
    share_ref,
    out_ref,
    slots,
    stage,
    one_list,
    other_list,
    sems,
):
    step = pl.program_id(0)
    half = out_ref.shape[0]
    cells = stage.shape[1]
    depth = CHUNK // cells

    @pl.when(step == 0)
    def _():
        def clear(block, carry):
            slots[pl.ds(pl.multiple_of(block * 256, 256), 256), :] = jnp.zeros((256, LANES), F32)
            return carry

        lax.fori_loop(0, 2 * half // 256, clear, 0)

    for q, strip in enumerate(conv_strips(padded_ref, taps_ref, *place_of(ny))):
        projected = jnp.dot(strip.astype(BF16), proj_ref[...], preferred_element_type=F32)
        stage[q] = projected * column_of(share_ref[q])

    def lay(which, slot):
        for cell in range(cells):
            row = stage[which, cell : cell + 1, :]
            for k in range(depth):
                slots[pl.ds(slot[k * cells + cell], 1), :] = row

    chunks_of(slot_ref, (one_list, other_list), sems, step, lay)

    @pl.when(step == pl.num_programs(0) - 1)
    def _():
        left = left_lanes(256)

        def pack(block, carry):
            at = pl.multiple_of(block * 256, 256)
            both = jnp.where(left, slots[pl.ds(at, 256), :], slots[pl.ds(half + at, 256), :])
            out_ref[pl.ds(at, 256), :] = both.astype(BF16)
            return carry

        lax.fori_loop(0, half // 256, pack, 0)


def spread(slot, padded, taps, proj, share, half):
    nx, ny, cells = padded.shape[0] - 2, padded.shape[1] - 2, padded.shape[2]
    return pl.pallas_call(
        functools.partial(spread_kernel, ny),
        grid=(nx * ny // 2,),
        out_shape=jax.ShapeDtypeStruct((half, LANES), BF16),
        in_specs=[
            whole(pl.ANY),
            whole(),
            whole(),
            whole(),
            pl.BlockSpec((2, 1, cells), lambda s: (s, 0, 0)),
        ],
        out_specs=whole(),
        scratch_shapes=[
            pltpu.VMEM((2 * half + 8, LANES), F32),
            pltpu.VMEM((2, cells, LANES), F32),
            *LISTS,
        ],
        compiler_params=params(),
        name="spread",
    )(slot, padded, taps, proj, share)


def settle_kernel(asked_ref, arrived_ref, out_ref, *scratch):
    sums, (stage, one_list, other_list, sems) = scratch[:-4], scratch[-4:]
    step = pl.program_id(0)
    per_step = arrived_ref.shape[0]
    points = out_ref.shape[1]

    @pl.when(step == 0)
    def _():
        def clear(block, carry):
            for total in sums:
                total[pl.ds(pl.multiple_of(block * LANES, LANES), LANES), :] = jnp.zeros(
                    (LANES, LANES), F32
                )
            return carry

        lax.fori_loop(0, (SPARE + points) // LANES, clear, 0)

    left = left_lanes()
    right = jnp.logical_not(left)
    ways = len(sums)
    def add(which, asked):
        for part in range(CHUNK // (2 * LANES)):
            at = part * 2 * LANES
            stage[part] = arrived_ref[which * (per_step // 2) + part].astype(F32)
            for row in range(LANES // ways):
                rows = [w * (LANES // ways) + row for w in range(ways)]
                ones = [pl.ds(asked[at + row], 1) for row in rows]
                twos = [pl.ds(asked[at + row + LANES], 1) for row in rows]
                values = [stage[part, row : row + 1, :] for row in rows]
                new_ones = [sums[w][ones[w], :] + values[w] for w in range(ways)]
                new_twos = [sums[w][twos[w], :] + values[w] for w in range(ways)]
                for w in range(ways):
                    pltpu.store(sums[w].at[ones[w], :], new_ones[w], mask=left)
                    pltpu.store(sums[w].at[twos[w], :], new_twos[w], mask=right)

    chunks_of(asked_ref, (one_list, other_list), sems, step, add)

    @pl.when(step == pl.num_programs(0) - 1)
    def _():
        def finish(block, carry):
            at = pl.multiple_of(block * LANES, LANES)
            rows = pl.ds(SPARE + at, LANES)
            total = sums[0][rows, :]
            for other in sums[1:]:
                total = total + other[rows, :]
            turned = total.T
            out_ref[:, pl.ds(at, LANES)] = turned[: LANES // 2] + turned[LANES // 2 :]
            return carry

        lax.fori_loop(0, points // LANES, finish, 0, unroll=2)


def settle(asked, arrived, points):
    sources = arrived.shape[0]
    per_step = 2 * CHUNK // (2 * LANES)
    return pl.pallas_call(
        settle_kernel,
        grid=(sources // per_step,),
        out_shape=jax.ShapeDtypeStruct((LANES // 2, points), F32),
        in_specs=[
            whole(pl.ANY),
            pl.BlockSpec((per_step, LANES, LANES), lambda s: (s, 0, 0)),
        ],
        out_specs=whole(),
        scratch_shapes=[pltpu.VMEM((SPARE + points, LANES), F32)] * 4
        + [pltpu.VMEM((per_step // 2, LANES, LANES), F32), *LISTS],
        compiler_params=params(),
        name="settle",
    )(asked, arrived)


def rims_of(shard, axis, dim):
    size, length = lax.axis_size(axis), shard.shape[dim]
    up = [(i, i + 1) for i in range(size - 1)]
    down = [(j, i) for i, j in up]
    before = lax.ppermute(lax.slice_in_dim(shard, length - 1, length, axis=dim), axis, up)
    after = lax.ppermute(lax.slice_in_dim(shard, 0, 1, axis=dim), axis, down)
    return before, after


def twice(matrix):
    wide = jnp.concatenate([matrix, matrix], axis=1)
    return jnp.concatenate([wide, jnp.zeros_like(wide)], axis=0)


def flipped(kernel):
    return jnp.flip(kernel, (2, 3, 4)).transpose(1, 0, 2, 3, 4)


def shards(
    point_features, neighbour_rows, neighbour_owner, valid, proj, kernel_one, kernel_two, cotangent
):
    channels, points = point_features.shape
    depth, nx, ny, cells = neighbour_rows.shape
    strips = nx * ny
    size_x, size_y = lax.axis_size("gx"), lax.axis_size("gy")
    devices = size_x * size_y
    cap = depth * strips * cells // devices
    half = devices * LANES

    def swap(array):
        return lax.all_to_all(array, ("gx", "gy"), split_axis=0, concat_axis=0, tiled=True)

    flat = (depth * strips, cells)
    slot, wanted = route(
        neighbour_owner.reshape(flat), neighbour_rows.reshape(flat), valid.reshape(flat), strips, devices, cap
    )
    slot = slot.reshape(-1)
    used = jnp.sum(valid.reshape(depth, strips, 1, cells), axis=0)
    share = 1.0 / jnp.maximum(used, 1).astype(F32)

    x_rims = rims_of(cotangent, "gx", 1)
    wanted, x_rims = lax.optimization_barrier((wanted, x_rims))
    asked = swap(wanted).reshape(-1)
    served = serve(asked, table_of(point_features))
    low, high = (
        jnp.concatenate([part[:, :, at : at + 1] for part in (x_rims[0], cotangent, x_rims[1])], 1)
        for at in (0, ny - 1)
    )
    y_rims = rims_of(jnp.concatenate([low, high], axis=2), "gy", 2)
    served, y_rims = lax.optimization_barrier((served, y_rims))
    got = swap(served)

    upward = jnp.concatenate([x_rims[0], cotangent, x_rims[1]], axis=1)
    upward = jnp.concatenate([y_rims[0], upward, y_rims[1]], axis=2)
    upward = upward.transpose(1, 2, 3, 0)
    upward = jnp.concatenate([upward, upward], axis=-1)
    upstream = upstream_of(upward, taps_of(flipped(kernel_two)))

    sizes = (size_x, size_y)
    latent = collect(sizes, nx, ny, slot, got.reshape(half, LANES), share, twice(proj))
    gated_grad = gated(sizes, latent, taps_of(kernel_one), upstream)
    outgoing = spread(slot, gated_grad, taps_of(flipped(kernel_one)), twice(proj.T), share, half)
    arrived = swap(outgoing.reshape(devices, LANES, LANES))
    return settle(asked, arrived, points)


def solution(mesh):
    placed = (
        P(None, ("gx", "gy")),
        P(None, "gx", "gy", None),
        P(None, "gx", "gy", None),
        P(None, "gx", "gy", None),
        P(),
        P(),
        P(),
        P(None, "gx", "gy", None),
    )
    return jax.shard_map(
        shards, mesh=mesh, in_specs=placed, out_specs=P(None, ("gx", "gy")), check_vma=False
    )
```

```python
import functools

import jax
import jax.numpy as jnp
from jax import lax
from jax.experimental import pallas as pl
from jax.experimental.pallas import tpu as pltpu
from jax.sharding import PartitionSpec as P

MESH = pl.DeviceIdType.MESH
SCALE_ROOT = 0.7978845608
CUBIC_TERM = 0.044715
LANES = 128
SPARE = 128
F32, BF16, I32 = jnp.float32, jnp.bfloat16, jnp.int32


def whole(space=pltpu.VMEM):
    return pl.BlockSpec(memory_space=space)


def params(mebibytes=60, **more):
    return pltpu.CompilerParams(vmem_limit_bytes=mebibytes * 1024 * 1024, **more)


def left_lanes(rows=1):
    return lax.broadcasted_iota(I32, (rows, LANES), 1) < LANES // 2


PART = LANES // 2
CHUNK = 1024


def chunks_of(list_ref, held, sems, step, work, order=lambda step: step):
    def copy(which, step):
        start = pl.multiple_of((2 * order(step) + which) * CHUNK, CHUNK)
        return pltpu.make_async_copy(list_ref.at[pl.ds(start, CHUNK)], held[which], sems.at[which])

    @pl.when(step == 0)
    def _():
        for which in range(2):
            copy(which, 0).start()

    for which in range(2):
        copy(which, step).wait()
        work(which, held[which])

        @pl.when(step < pl.num_programs(0) - 1)
        def _():
            copy(which, step + 1).start()


LISTS = [pltpu.SMEM((CHUNK,), I32), pltpu.SMEM((CHUNK,), I32), pltpu.SemaphoreType.DMA((2,))]


def route_kernel(strips, owner_ref, rows_ref, valid_ref, slot_ref, want_ref, sums):
    blocks, width = owner_ref.shape
    owners, cap = want_ref.shape
    trash = owners * cap
    together = 4
    owner_of = lax.broadcasted_iota(I32, (owners, width), 0).astype(F32).astype(BF16)
    rank_of = lax.broadcasted_iota(I32, (cap, width), 0).astype(F32).astype(BF16)
    first = lax.broadcasted_iota(I32, (width, 2 * width), 0)
    second = lax.broadcasted_iota(I32, (width, 2 * width), 1)
    earlier = jnp.where((second >= width) | (first < second), 1.0, 0.0).astype(BF16)
    one, zero = jnp.ones((), BF16), jnp.zeros((), BF16)
    sums[...] = jnp.zeros_like(sums)

    def body(group, offset):
        pieces, at_rank = [], []
        for part in range(together):
            block = group * together + part
            owner = owner_ref[pl.ds(block, 1), :]
            rows = rows_ref[pl.ds(block, 1), :]
            used = valid_ref[pl.ds(block, 1), :] > 0
            hit = owner_of == jnp.where(used, owner, -1).astype(F32).astype(BF16)
            chosen = jnp.where(hit, one, zero)
            counts = jnp.dot(chosen, earlier, preferred_element_type=F32)
            before = (counts[:, :width] + offset).astype(BF16)
            offset = offset + counts[:, width:]
            rank = jnp.sum(jnp.where(hit, before, zero).astype(F32), axis=0, keepdims=True)
            at_rank.append(jnp.where(rank_of == rank.astype(BF16), one, zero))
            rank = rank.astype(I32)
            place = (rank >> 7) * (owners * LANES) + owner * LANES + (rank & 127)
            at = block % strips * (blocks // strips) + block // strips
            slot_ref[pl.ds(at, 1), :] = jnp.where(used, place, trash)
            high = ((rows >> 7) + 1).astype(F32).astype(BF16)
            low = (rows & 127).astype(F32).astype(BF16)
            pieces.append(
                jnp.concatenate([jnp.where(hit, high, zero), jnp.where(hit, low, zero)], axis=0)
            )
        sums[...] += lax.dot_general(
            jnp.concatenate(pieces, axis=1),
            jnp.concatenate(at_rank, axis=1),
            (((1,), (1,)), ((), ())),
            preferred_element_type=F32,
        )
        return offset

    lax.fori_loop(0, blocks // together, body, jnp.zeros((owners, width), F32))
    want_ref[...] = (sums[:owners, :] * 128.0 + sums[owners:, :]).astype(I32)


def route(owner, rows, valid, strips, owners, cap):
    blocks, width = owner.shape
    return pl.pallas_call(
        functools.partial(route_kernel, strips),
        out_shape=(
            jax.ShapeDtypeStruct((blocks, width), I32),
            jax.ShapeDtypeStruct((owners, cap), I32),
        ),
        in_specs=[whole()] * 3,
        out_specs=(whole(), whole()),
        scratch_shapes=[pltpu.VMEM((2 * owners, cap), F32)],
        compiler_params=params(16),
        name="route",
    )(owner, rows, valid)


def table_kernel(features_ref, out_ref):
    points = features_ref.shape[1]
    out_ref[:SPARE, :] = jnp.zeros((SPARE, LANES), BF16)

    def fill(block, carry):
        at = pl.multiple_of(block * LANES, LANES)
        part = features_ref[:, pl.ds(at, LANES)]
        both = jnp.concatenate([part, part], axis=0).T
        out_ref[pl.ds(SPARE + at, LANES), :] = both.astype(BF16)
        return carry

    lax.fori_loop(0, points // LANES, fill, 0, unroll=8)


def table_of(features):
    channels, points = features.shape
    return pl.pallas_call(
        table_kernel,
        out_shape=jax.ShapeDtypeStruct((SPARE + points, LANES), BF16),
        in_specs=[whole()],
        out_specs=whole(),
        compiler_params=params(16),
        cost_estimate=pl.CostEstimate(flops=0, bytes_accessed=32 << 20, transcendentals=0),
        name="table",
    )(features)


def serve_kernel(asked_ref, table_ref, out_ref, table, stage, one_list, other_list, sems):
    step = pl.program_id(0)
    held = (one_list, other_list)
    per_step = out_ref.shape[0]

    @pl.when(step == 0)
    def _():
        def widen(block, carry):
            rows = pl.ds(pl.multiple_of(block * LANES, LANES), LANES)
            table[rows, :] = table_ref[rows, :].astype(F32)
            return carry

        lax.fori_loop(0, table.shape[0] // LANES, widen, 0, unroll=3)

    left = left_lanes()

    def gather(which, asked):
        for block in range(CHUNK // (2 * LANES)):
            at = block * 2 * LANES
            for row in range(LANES):
                one = table[pl.ds(asked[at + row], 1), :]
                two = table[pl.ds(asked[at + row + LANES], 1), :]
                stage[block, row : row + 1, :] = jnp.where(left, one, two)
            out_ref[which * (per_step // 2) + block] = stage[block].astype(BF16)

    chunks_of(asked_ref, held, sems, step, gather)


def serve(asked, table):
    sources = asked.shape[0] // (2 * LANES)
    per_step = 2 * CHUNK // (2 * LANES)
    return pl.pallas_call(
        serve_kernel,
        grid=(sources // per_step,),
        out_shape=jax.ShapeDtypeStruct((sources, LANES, LANES), BF16),
        in_specs=[whole(pl.ANY), whole()],
        out_specs=pl.BlockSpec((per_step, LANES, LANES), lambda s: (s, 0, 0)),
        scratch_shapes=[
            pltpu.VMEM(table.shape, F32),
            pltpu.VMEM((per_step // 2, LANES, LANES), F32),
            *LISTS,
        ],
        compiler_params=params(24),
        cost_estimate=pl.CostEstimate(flops=0, bytes_accessed=32 << 20, transcendentals=0),
        name="serve",
    )(asked, table)


AROUND = ((1, 0), (-1, 0), (1, 1), (1, -1), (-1, 1), (-1, -1), (0, 1), (0, -1))
X_SENDS, Y_SENDS = range(6), range(6, 8)


def rim_first(nx, ny, step):
    pairs = ny // 2
    late = step // (2 * pairs)
    at = step - 2 * pairs
    inner = nx - 2
    ends = at // (2 * inner)
    first = (step // pairs) * (nx - 1) * pairs + step % pairs
    end = (1 + at // 2) * pairs + (at % 2) * (pairs - 1)
    rest = at - 2 * inner
    middle = (1 + rest // (pairs - 2)) * pairs + 1 + rest % (pairs - 2)
    return (1 - late) * first + late * ((1 - ends) * end + ends * middle)


def rim_steps(nx, ny):
    return ny - 1, ny - 1 + 2 * (nx - 2)


class Rims:
    def __init__(self, sizes, out_ref, send_x, send_y, send_c, come_x, come_y, come_c, sent, come):
        self.sizes, self.out = sizes, out_ref
        self.at = (lax.axis_index("gx"), lax.axis_index("gy"))
        self.nx, self.ny = out_ref.shape[0] - 2, out_ref.shape[1] - 2
        self.cells = out_ref.shape[2]
        self.send, self.come = (send_x, send_y, send_c), (come_x, come_y, come_c)
        self.sems = (sent, come)

    def device(self, di, dj):
        (i, j), (size_x, size_y) = self.at, self.sizes
        return (lax.rem(i + di + size_x, size_x), lax.rem(j + dj + size_y, size_y))

    def copy(self, number):
        kind, at = (0, number) if number < 2 else (2, number - 2) if number < 6 else (1, number - 6)
        return pltpu.make_async_remote_copy(
            src_ref=self.send[kind].at[at],
            dst_ref=self.come[kind].at[at],
            send_sem=self.sems[0].at[number],
            recv_sem=self.sems[1].at[number],
            device_id=self.device(*AROUND[number]),
            device_id_type=MESH,
        )

    def greet(self):
        barrier = pltpu.get_barrier_semaphore()
        for di, dj in AROUND:
            pl.semaphore_signal(barrier, inc=1, device_id=self.device(di, dj), device_id_type=MESH)

    def send_first(self):
        pl.semaphore_wait(pltpu.get_barrier_semaphore(), len(AROUND))
        left = left_lanes(self.cells)
        deep = self.cells // 2
        for number in X_SENDS:
            di, dj = AROUND[number]
            x = self.nx if di > 0 else 1
            if dj == 0:
                for q in range(self.ny // 2):
                    self.send[0][number, q] = jnp.where(
                        left, self.out[x, 2 * q + 1], self.out[x, 2 * q + 2]
                    )
            else:
                row = self.out.at[x, self.ny if dj > 0 else 1]
                self.send[2][number - 2] = jnp.where(left[:deep], row[:deep, :], row[deep:, :])
            self.copy(number).start()

    def send_last(self):
        left = left_lanes(self.cells)
        for number in Y_SENDS:
            y = self.ny if AROUND[number][1] > 0 else 1
            for q in range(self.nx // 2):
                self.send[1][number - 6, q] = jnp.where(
                    left, self.out[2 * q + 1, y], self.out[2 * q + 2, y]
                )
            self.copy(number).start()

    def finish(self):
        left = left_lanes(self.cells)
        deep = self.cells // 2
        (i, j), (size_x, size_y) = self.at, self.sizes
        come_x, come_y, come_c = self.come

        def apart(both, keep):
            both = jnp.where(keep, both.astype(F32), 0.0)
            turned = pltpu.roll(both, LANES // 2, 1)
            side = left[: both.shape[0]]
            return (
                jnp.where(side, both, turned).astype(BF16),
                jnp.where(side, turned, both).astype(BF16),
            )

        for number, (di, dj) in enumerate(AROUND):
            self.copy(number).wait()
            keep_x = (i > 0) if di > 0 else (i < size_x - 1)
            keep_y = (j > 0) if dj > 0 else (j < size_y - 1)
            x = 0 if di > 0 else self.nx + 1
            y = 0 if dj > 0 else self.ny + 1
            if dj == 0:
                for q in range(self.ny // 2):
                    for p, row in enumerate(apart(come_x[number, q], keep_x)):
                        self.out[x, 2 * q + p + 1] = row
            elif di == 0:
                for q in range(self.nx // 2):
                    for p, row in enumerate(apart(come_y[number - 6, q], keep_y)):
                        self.out[2 * q + p + 1, y] = row
            else:
                place = self.out.at[x, y]
                for p, row in enumerate(apart(come_c[number - 2], keep_x & keep_y)):
                    place[p * deep : (p + 1) * deep, :] = row

    def around(self, step, work):
        first, last = rim_steps(self.nx, self.ny)

        @pl.when(step == 0)
        def _():
            self.greet()

        work()

        @pl.when(step == first)
        def _():
            self.send_first()

        @pl.when(step == last)
        def _():
            self.send_last()

        @pl.when(step == pl.num_programs(0) - 1)
        def _():
            self.finish()


def rim_scratch(nx, ny, cells):
    def buffers():
        return [
            pltpu.VMEM((2, ny // 2, cells, LANES), BF16),
            pltpu.VMEM((2, nx // 2, cells, LANES), BF16),
            pltpu.VMEM((4, cells // 2, LANES), BF16),
        ]

    return [*buffers(), *buffers(), pltpu.SemaphoreType.DMA((8,)), pltpu.SemaphoreType.DMA((8,))]


def column_of(row):
    return jnp.broadcast_to(row, (LANES, row.shape[1])).T


def collect_kernel(
    sizes,
    slot_ref,
    got_ref,
    share_ref,
    proj_ref,
    out_ref,
    table,
    stage,
    one_list,
    other_list,
    sems,
    *rim_refs,
):
    step = pl.program_id(0)
    nx, ny = out_ref.shape[0] - 2, out_ref.shape[1] - 2
    order = functools.partial(rim_first, nx, ny)
    pair = order(step)
    x, y = pair // (ny // 2), pair % (ny // 2) * 2
    half = got_ref.shape[0] * LANES
    cells = stage.shape[1]
    depth = CHUNK // cells

    @pl.when(step == 0)
    def _():
        left = left_lanes(LANES)

        def fill(owner, carry):
            at = pl.multiple_of(owner * LANES, LANES)
            rows = got_ref[owner].astype(F32)
            table[pl.ds(at, LANES), :] = jnp.where(left, rows, 0.0)
            table[pl.ds(half + at, LANES), :] = jnp.where(left, 0.0, rows)
            return carry

        lax.fori_loop(0, half // LANES, fill, 0, unroll=4)
        table[2 * half :, :] = jnp.zeros((8, LANES), F32)

    def gather(which, slot):
        for cell in range(cells):
            total = table[pl.ds(slot[cell], 1), :]
            for k in range(1, depth):
                total = total + table[pl.ds(slot[k * cells + cell], 1), :]
            stage[which, cell : cell + 1, :] = total
        total = stage[which]
        total = total + pltpu.roll(total, LANES // 2, 1)
        averaged = (total * column_of(share_ref[which])).astype(BF16)
        latent = jnp.dot(averaged, proj_ref[...], preferred_element_type=F32).astype(BF16)
        out_ref[x + 1, y + which + 1] = latent

    def work():
        chunks_of(slot_ref, (one_list, other_list), sems, step, gather, order)

    Rims(sizes, out_ref, *rim_refs).around(step, work)


def collect(sizes, nx, ny, slot, got, share, proj):
    strips, _, cells = share.shape
    half = got.shape[0] * LANES
    return pl.pallas_call(
        functools.partial(collect_kernel, sizes),
        grid=(strips // 2,),
        out_shape=jax.ShapeDtypeStruct((nx + 2, ny + 2, cells, LANES), BF16),
        in_specs=[
            whole(pl.ANY),
            whole(),
            pl.BlockSpec((2, 1, cells), lambda s: (rim_first(nx, ny, s), 0, 0)),
            whole(),
        ],
        out_specs=whole(),
        scratch_shapes=[
            pltpu.VMEM((2 * half + 8, LANES), F32),
            pltpu.VMEM((2, cells, LANES), F32),
            *LISTS,
            *rim_scratch(nx, ny, cells),
        ],
        compiler_params=params(36, collective_id=0, has_side_effects=True),
        name="collect",
    )(slot, got, share, proj)


def gelu_slope(value):
    inner = SCALE_ROOT * (value + CUBIC_TERM * value * value * value)
    tangent = jnp.tanh(inner)
    return 0.5 * (1.0 + tangent) + 0.5 * value * (1.0 - tangent * tangent) * SCALE_ROOT * (
        1.0 + 3.0 * CUBIC_TERM * value * value
    )


def taps_of(kernel):
    o, i = kernel.shape[:2]
    taps = kernel.transpose(2, 3, 1, 4, 0)
    taps = jnp.concatenate([taps, jnp.zeros((3, 1, i, 3, o), taps.dtype)], axis=1)
    order = [taps[..., c, :] for c in (1, 0, 2, 1)]
    return jnp.concatenate(order, axis=-1).reshape(12 * i, 4 * o)


def conv_strips(padded_ref, taps_ref, x, y):
    cells = padded_ref.shape[2]
    left = left_lanes(cells)
    strips = []
    for q in range(2):
        parts = []
        for a in range(3):
            parts.append(jnp.where(left, padded_ref[x + a, y + q], padded_ref[x + a, y + q + 1]))
            parts.append(padded_ref[x + a, y + q + 2])
        strips.append(jnp.concatenate(parts, axis=1))
    sums = jnp.dot(jnp.concatenate(strips, axis=0), taps_ref[...], preferred_element_type=F32)
    depth = lax.broadcasted_iota(I32, (cells, LANES), 0)
    results = []
    for q in range(2):
        one = sums[q * cells : (q + 1) * cells, :LANES]
        two = sums[q * cells : (q + 1) * cells, LANES:]
        below = jnp.where(depth == 0, 0.0, pltpu.roll(one, 1, 0))
        above = jnp.where(depth == cells - 1, 0.0, pltpu.roll(two, cells - 1, 0))
        sides = jnp.where(left, above, below)
        here = jnp.where(left, one, two)
        results.append(here + sides + pltpu.roll(sides, LANES // 2, 1))
    return results


def place_of(ny):
    first = 2 * pl.program_id(0)
    return first // ny, first % ny


def upstream_kernel(ny, padded_ref, taps_ref, out_ref):
    for q, strip in enumerate(conv_strips(padded_ref, taps_ref, *place_of(ny))):
        out_ref[q] = strip


def gate_kernel(sizes, padded_ref, taps_ref, upstream_ref, out_ref, *rim_refs):
    step = pl.program_id(0)
    nx, ny = out_ref.shape[0] - 2, out_ref.shape[1] - 2
    pair = rim_first(nx, ny, step)
    x, y = pair // (ny // 2), pair % (ny // 2) * 2

    def work():
        for q, preact in enumerate(conv_strips(padded_ref, taps_ref, x, y)):
            gated_grad = (upstream_ref[q] * gelu_slope(preact)).astype(BF16)
            out_ref[x + 1, y + q + 1] = gated_grad

    Rims(sizes, out_ref, *rim_refs).around(step, work)


def strip_spec(cells):
    return pl.BlockSpec((2, cells, LANES), lambda s: (s, 0, 0))


def conv_cost(strips, cells):
    return pl.CostEstimate(
        flops=2 * strips * cells * 12 * 64 * 4 * 64, bytes_accessed=12 << 20, transcendentals=0
    )


def upstream_of(padded, taps):
    nx, ny, cells = padded.shape[0] - 2, padded.shape[1] - 2, padded.shape[2]
    return pl.pallas_call(
        functools.partial(upstream_kernel, ny),
        grid=(nx * ny // 2,),
        out_shape=jax.ShapeDtypeStruct((nx * ny, cells, LANES), F32),
        in_specs=[whole(), whole()],
        out_specs=strip_spec(cells),
        compiler_params=params(24),
        cost_estimate=conv_cost(nx * ny, cells),
        name="upstream",
    )(padded, taps)


def gated(sizes, padded, taps, upstream):
    nx, ny, cells = padded.shape[0] - 2, padded.shape[1] - 2, padded.shape[2]
    return pl.pallas_call(
        functools.partial(gate_kernel, sizes),
        grid=(nx * ny // 2,),
        out_shape=jax.ShapeDtypeStruct(padded.shape, BF16),
        in_specs=[
            whole(),
            whole(),
            pl.BlockSpec((2, cells, LANES), lambda s: (rim_first(nx, ny, s), 0, 0)),
        ],
        out_specs=whole(),
        scratch_shapes=rim_scratch(nx, ny, cells),
        compiler_params=params(24, collective_id=1, has_side_effects=True),
        cost_estimate=conv_cost(nx * ny, cells),
        name="gated",
    )(padded, taps, upstream)


def spread_kernel(
    ny,
    slot_ref,
    padded_ref,
    taps_ref,
    proj_ref,
    share_ref,
    one_ref,
    two_ref,
    slots,
    stage,
    one_list,
    other_list,
    sems,
):
    step = pl.program_id(0)
    half = slots.shape[0] // 2 // LANES * LANES
    cells = stage.shape[1]
    depth = CHUNK // cells

    @pl.when(step == 0)
    def _():
        def clear(block, carry):
            slots[pl.ds(pl.multiple_of(block * 256, 256), 256), :] = jnp.zeros((256, LANES), F32)
            return carry

        lax.fori_loop(0, 2 * half // 256, clear, 0)

    for q, strip in enumerate(conv_strips(padded_ref, taps_ref, *place_of(ny))):
        projected = jnp.dot(strip.astype(BF16), proj_ref[...], preferred_element_type=F32)
        stage[q] = projected * column_of(share_ref[q])

    def lay(which, slot):
        for cell in range(cells):
            row = stage[which, cell : cell + 1, :]
            for k in range(depth):
                slots[pl.ds(slot[k * cells + cell], 1), :] = row

    chunks_of(slot_ref, (one_list, other_list), sems, step, lay)

    @pl.when(step == pl.num_programs(0) - 1)
    def _():
        left = left_lanes(LANES)

        def pack(owner, carry):
            at = pl.multiple_of(owner * LANES, LANES)
            both = jnp.where(left, slots[pl.ds(at, LANES), :], slots[pl.ds(half + at, LANES), :])
            both = both.astype(BF16)
            one_ref[owner] = both[:PART]
            two_ref[owner] = both[PART:]
            return carry

        lax.fori_loop(0, half // LANES, pack, 0, unroll=2)


def spread(slot, padded, taps, proj, share, half):
    nx, ny, cells = padded.shape[0] - 2, padded.shape[1] - 2, padded.shape[2]
    return pl.pallas_call(
        functools.partial(spread_kernel, ny),
        grid=(nx * ny // 2,),
        out_shape=(jax.ShapeDtypeStruct((half // LANES, PART, LANES), BF16),) * 2,
        in_specs=[
            whole(pl.ANY),
            whole(),
            whole(),
            whole(),
            pl.BlockSpec((2, 1, cells), lambda s: (s, 0, 0)),
        ],
        out_specs=(whole(), whole()),
        scratch_shapes=[
            pltpu.VMEM((2 * half + 8, LANES), F32),
            pltpu.VMEM((2, cells, LANES), F32),
            *LISTS,
        ],
        compiler_params=params(36),
        name="spread",
    )(slot, padded, taps, proj, share)


def add_rows(asked_ref, arrived_ref, sums, stage, lists, part):
    left = left_lanes()
    right = jnp.logical_not(left)

    def store(totals, places, values):
        for total, (one, two), (new_one, new_two) in zip(totals, places, values):
            pltpu.store(total.at[one, :], new_one, mask=left)
            pltpu.store(total.at[two, :], new_two, mask=right)

    def add(which, asked):
        waiting = None
        for block in range(CHUNK // (2 * LANES)):
            at = block * 2 * LANES + part * PART
            stage[block] = arrived_ref[which * (CHUNK // (2 * LANES)) + block].astype(F32)
            for group in range(PART // 2):
                totals = sums[:2] if group % 2 == 0 else sums[2:]
                places, values = [], []
                for total, row in zip(totals, (2 * group, 2 * group + 1)):
                    one, two = pl.ds(asked[at + row], 1), pl.ds(asked[at + row + LANES], 1)
                    value = stage[block, row : row + 1, :]
                    places.append((one, two))
                    values.append((total[one, :] + value, total[two, :] + value))
                if waiting is not None:
                    store(*waiting)
                waiting = (totals, places, values)
        store(*waiting)

    chunks_of(asked_ref, lists[:2], lists[2], pl.program_id(0), add)


def clear_sums(sums):
    def clear(block, carry):
        for total in sums:
            total[pl.ds(pl.multiple_of(block * LANES, LANES), LANES), :] = jnp.zeros(
                (LANES, LANES), F32
            )
        return carry

    lax.fori_loop(0, sums[0].shape[0] // LANES, clear, 0)


def first_kernel(asked_ref, arrived_ref, out_ref, one, two, three, stage, *lists):
    step = pl.program_id(0)
    sums = (out_ref, one, two, three)

    @pl.when(step == 0)
    def _():
        clear_sums(sums)

    add_rows(asked_ref, arrived_ref, sums, stage, lists, 0)

    @pl.when(step == pl.num_programs(0) - 1)
    def _():
        def finish(block, carry):
            rows = pl.ds(pl.multiple_of(block * LANES, LANES), LANES)
            out_ref[rows, :] = (out_ref[rows, :] + one[rows, :]) + (two[rows, :] + three[rows, :])
            return carry

        lax.fori_loop(0, out_ref.shape[0] // LANES, finish, 0)


def last_kernel(asked_ref, arrived_ref, before_ref, out_ref, *scratch):
    sums, (held, sem, stage, *lists) = scratch[:4], scratch[4:]
    step = pl.program_id(0)
    points = out_ref.shape[1]

    def fetch():
        return pltpu.make_async_copy(before_ref, held, sem)

    @pl.when(step == 0)
    def _():
        fetch().start()
        clear_sums(sums)

    add_rows(asked_ref, arrived_ref, sums, stage, lists, 1)

    @pl.when(step == pl.num_programs(0) - 1)
    def _():
        fetch().wait()

        def finish(block, carry):
            at = pl.multiple_of(block * LANES, LANES)
            rows = pl.ds(SPARE + at, LANES)
            total = held[rows, :]
            for other in sums:
                total = total + other[rows, :]
            turned = total.T
            out_ref[:, pl.ds(at, LANES)] = turned[: LANES // 2] + turned[LANES // 2 :]
            return carry

        lax.fori_loop(0, points // LANES, finish, 0, unroll=8)


def settle_specs(arrived):
    per_step = 2 * CHUNK // (2 * LANES)
    grid = (arrived.shape[0] // per_step,)
    specs = [whole(pl.ANY), pl.BlockSpec((per_step, PART, LANES), lambda s: (s, 0, 0))]
    return grid, specs, [pltpu.VMEM((per_step // 2, PART, LANES), F32), *LISTS]


def settle_first(asked, arrived, points):
    grid, specs, scratch = settle_specs(arrived)
    return pl.pallas_call(
        first_kernel,
        grid=grid,
        out_shape=jax.ShapeDtypeStruct((SPARE + points, LANES), F32),
        in_specs=specs,
        out_specs=whole(),
        scratch_shapes=[pltpu.VMEM((SPARE + points, LANES), F32)] * 3 + scratch,
        compiler_params=params(44),
        cost_estimate=pl.CostEstimate(flops=0, bytes_accessed=64 << 20, transcendentals=0),
        name="settle_first",
    )(asked, arrived)


def settle_last(asked, arrived, before, points):
    grid, specs, scratch = settle_specs(arrived)
    return pl.pallas_call(
        last_kernel,
        grid=grid,
        out_shape=jax.ShapeDtypeStruct((LANES // 2, points), F32),
        in_specs=[*specs, whole(pl.ANY)],
        out_specs=whole(),
        scratch_shapes=[pltpu.VMEM((SPARE + points, LANES), F32)] * 5
        + [pltpu.SemaphoreType.DMA(())]
        + scratch,
        compiler_params=params(56),
        name="settle_last",
    )(asked, arrived, before)


def rims_of(shard, axis, dim):
    size, length = lax.axis_size(axis), shard.shape[dim]
    up = [(i, i + 1) for i in range(size - 1)]
    down = [(j, i) for i, j in up]
    before = lax.ppermute(lax.slice_in_dim(shard, length - 1, length, axis=dim), axis, up)
    after = lax.ppermute(lax.slice_in_dim(shard, 0, 1, axis=dim), axis, down)
    return before, after


def twice(matrix):
    wide = jnp.concatenate([matrix, matrix], axis=1)
    return jnp.concatenate([wide, jnp.zeros_like(wide)], axis=0)


def flipped(kernel):
    return jnp.flip(kernel, (2, 3, 4)).transpose(1, 0, 2, 3, 4)


def shards(
    point_features, neighbour_rows, neighbour_owner, valid, proj, kernel_one, kernel_two, cotangent
):
    channels, points = point_features.shape
    depth, nx, ny, cells = neighbour_rows.shape
    strips = nx * ny
    size_x, size_y = lax.axis_size("gx"), lax.axis_size("gy")
    devices = size_x * size_y
    cap = depth * strips * cells // devices
    half = devices * LANES

    def swap(array):
        return lax.all_to_all(array, ("gx", "gy"), split_axis=0, concat_axis=0, tiled=True)

    flat = (depth * strips, cells)
    slot, wanted = route(
        neighbour_owner.reshape(flat), neighbour_rows.reshape(flat), valid.reshape(flat), strips, devices, cap
    )
    slot = slot.reshape(-1)
    used = jnp.sum(valid.reshape(depth, strips, 1, cells), axis=0)
    share = 1.0 / jnp.maximum(used, 1).astype(F32)

    x_rims = rims_of(cotangent, "gx", 1)
    wanted, x_rims = lax.optimization_barrier((wanted, x_rims))
    asked = swap(wanted).reshape(-1)
    table = table_of(point_features)
    served = serve(asked, table)
    low, high = (
        jnp.concatenate([part[:, :, at : at + 1] for part in (x_rims[0], cotangent, x_rims[1])], 1)
        for at in (0, ny - 1)
    )
    y_rims = rims_of(jnp.concatenate([low, high], axis=2), "gy", 2)
    served, y_rims = lax.optimization_barrier((served, y_rims))
    got = swap(served)

    upward = jnp.concatenate([x_rims[0], cotangent, x_rims[1]], axis=1)
    upward = jnp.concatenate([y_rims[0], upward, y_rims[1]], axis=2)
    upward = upward.transpose(1, 2, 3, 0)
    upward = jnp.concatenate([upward, upward], axis=-1)
    upstream = upstream_of(upward, taps_of(flipped(kernel_two)))

    sizes = (size_x, size_y)
    latent = collect(sizes, nx, ny, slot, got, share, twice(proj))
    gated_grad = gated(sizes, latent, taps_of(kernel_one), upstream)
    one, two = spread(slot, gated_grad, taps_of(flipped(kernel_one)), twice(proj.T), share, half)
    one = swap(one)
    one, two = lax.optimization_barrier((one, two))
    two = swap(two)
    return settle_last(asked, two, settle_first(asked, one, points), points)


def solution(mesh):
    placed = (
        P(None, ("gx", "gy")),
        P(None, "gx", "gy", None),
        P(None, "gx", "gy", None),
        P(None, "gx", "gy", None),
        P(),
        P(),
        P(),
        P(None, "gx", "gy", None),
    )
    return jax.shard_map(
        shards, mesh=mesh, in_specs=placed, out_specs=P(None, ("gx", "gy")), check_vma=False
    )
```

```python
import functools

import jax
import jax.numpy as jnp
from jax import lax
from jax.experimental import pallas as pl
from jax.experimental.pallas import tpu as pltpu
from jax.sharding import PartitionSpec as P

MESH = pl.DeviceIdType.MESH
SCALE_ROOT = 0.7978845608
CUBIC_TERM = 0.044715
LANES = 128
SPARE = 128
F32, BF16, I32 = jnp.float32, jnp.bfloat16, jnp.int32


def whole(space=pltpu.VMEM):
    return pl.BlockSpec(memory_space=space)


def params(mebibytes=60, **more):
    return pltpu.CompilerParams(vmem_limit_bytes=mebibytes * 1024 * 1024, **more)


def left_lanes(rows=1):
    return lax.broadcasted_iota(I32, (rows, LANES), 1) < LANES // 2


PART = LANES // 2
CHUNK = 1024


def chunks_of(list_ref, held, sems, step, work, order=lambda step: step):
    def copy(which, step):
        start = pl.multiple_of((2 * order(step) + which) * CHUNK, CHUNK)
        return pltpu.make_async_copy(list_ref.at[pl.ds(start, CHUNK)], held[which], sems.at[which])

    @pl.when(step == 0)
    def _():
        for which in range(2):
            copy(which, 0).start()

    for which in range(2):
        copy(which, step).wait()
        work(which, held[which])

        @pl.when(step < pl.num_programs(0) - 1)
        def _():
            copy(which, step + 1).start()


LISTS = [pltpu.SMEM((CHUNK,), I32), pltpu.SMEM((CHUNK,), I32), pltpu.SemaphoreType.DMA((2,))]


def route_kernel(strips, owner_ref, rows_ref, valid_ref, slot_ref, want_ref, sums):
    blocks, width = owner_ref.shape
    owners, cap = want_ref.shape
    trash = owners * cap
    together = 8
    owner_of = lax.broadcasted_iota(I32, (owners, width), 0).astype(F32).astype(BF16)
    rank_of = lax.broadcasted_iota(I32, (cap, width), 0).astype(F32).astype(BF16)
    first = lax.broadcasted_iota(I32, (width, 2 * width), 0)
    second = lax.broadcasted_iota(I32, (width, 2 * width), 1)
    earlier = jnp.where((second >= width) | (first < second), 1.0, 0.0).astype(BF16)
    one, zero = jnp.ones((), BF16), jnp.zeros((), BF16)
    sums[...] = jnp.zeros_like(sums)

    def body(group, offset):
        pieces, at_rank = [], []
        blocks_here = [group * together + part for part in range(together)]
        uses, hits = [], []
        for block in blocks_here:
            uses.append(valid_ref[pl.ds(block, 1), :] > 0)
            owner = jnp.where(uses[-1], owner_ref[pl.ds(block, 1), :], -1)
            hits.append(owner_of == owner.astype(F32).astype(BF16))
        chosen = jnp.concatenate([jnp.where(hit, one, zero) for hit in hits], axis=0)
        counts_here = jnp.dot(chosen, earlier, preferred_element_type=F32)
        for part, (block, used, hit) in enumerate(zip(blocks_here, uses, hits)):
            owner = owner_ref[pl.ds(block, 1), :]
            rows = rows_ref[pl.ds(block, 1), :]
            counts = counts_here[part * owners : (part + 1) * owners, :]
            before = (counts[:, :width] + offset).astype(BF16)
            offset = offset + counts[:, width:]
            rank = jnp.sum(jnp.where(hit, before, zero).astype(F32), axis=0, keepdims=True)
            at_rank.append(jnp.where(rank_of == rank.astype(BF16), one, zero))
            rank = rank.astype(I32)
            place = (rank >> 7) * (owners * LANES) + owner * LANES + (rank & 127)
            at = block % strips * (blocks // strips) + block // strips
            slot_ref[pl.ds(at, 1), :] = jnp.where(used, place, trash)
            high = ((rows >> 7) + 1).astype(F32).astype(BF16)
            low = (rows & 127).astype(F32).astype(BF16)
            pieces.append(
                jnp.concatenate([jnp.where(hit, high, zero), jnp.where(hit, low, zero)], axis=0)
            )
        sums[...] += lax.dot_general(
            jnp.concatenate(pieces, axis=1),
            jnp.concatenate(at_rank, axis=1),
            (((1,), (1,)), ((), ())),
            preferred_element_type=F32,
        )
        return offset

    lax.fori_loop(0, blocks // together, body, jnp.zeros((owners, width), F32))
    want_ref[...] = (sums[:owners, :] * 128.0 + sums[owners:, :]).astype(I32)


def route(owner, rows, valid, strips, owners, cap):
    blocks, width = owner.shape
    return pl.pallas_call(
        functools.partial(route_kernel, strips),
        out_shape=(
            jax.ShapeDtypeStruct((blocks, width), I32),
            jax.ShapeDtypeStruct((owners, cap), I32),
        ),
        in_specs=[whole()] * 3,
        out_specs=(whole(), whole()),
        scratch_shapes=[pltpu.VMEM((2 * owners, cap), F32)],
        compiler_params=params(16),
        name="route",
    )(owner, rows, valid)


def table_kernel(features_ref, out_ref):
    points = features_ref.shape[1]
    out_ref[:SPARE, :] = jnp.zeros((SPARE, LANES), BF16)

    def fill(block, carry):
        at = pl.multiple_of(block * LANES, LANES)
        part = features_ref[:, pl.ds(at, LANES)]
        both = jnp.concatenate([part, part], axis=0).T
        out_ref[pl.ds(SPARE + at, LANES), :] = both.astype(BF16)
        return carry

    lax.fori_loop(0, points // LANES, fill, 0, unroll=8)


def table_of(features):
    channels, points = features.shape
    return pl.pallas_call(
        table_kernel,
        out_shape=jax.ShapeDtypeStruct((SPARE + points, LANES), BF16),
        in_specs=[whole()],
        out_specs=whole(),
        compiler_params=params(16),
        cost_estimate=pl.CostEstimate(flops=0, bytes_accessed=32 << 20, transcendentals=0),
        name="table",
    )(features)


def serve_kernel(asked_ref, table_ref, out_ref, table, stage, one_list, other_list, sems):
    step = pl.program_id(0)
    held = (one_list, other_list)
    per_step = out_ref.shape[0]

    @pl.when(step == 0)
    def _():
        def widen(block, carry):
            rows = pl.ds(pl.multiple_of(block * LANES, LANES), LANES)
            table[rows, :] = table_ref[rows, :].astype(F32)
            return carry

        lax.fori_loop(0, table.shape[0] // LANES, widen, 0, unroll=3)

    left = left_lanes()

    def gather(which, asked):
        for block in range(CHUNK // (2 * LANES)):
            at = block * 2 * LANES
            for row in range(LANES):
                one = table[pl.ds(asked[at + row], 1), :]
                two = table[pl.ds(asked[at + row + LANES], 1), :]
                stage[block, row : row + 1, :] = jnp.where(left, one, two)
            out_ref[which * (per_step // 2) + block] = stage[block].astype(BF16)

    chunks_of(asked_ref, held, sems, step, gather)


def serve(asked, table):
    sources = asked.shape[0] // (2 * LANES)
    per_step = 2 * CHUNK // (2 * LANES)
    return pl.pallas_call(
        serve_kernel,
        grid=(sources // per_step,),
        out_shape=jax.ShapeDtypeStruct((sources, LANES, LANES), BF16),
        in_specs=[whole(pl.ANY), whole()],
        out_specs=pl.BlockSpec((per_step, LANES, LANES), lambda s: (s, 0, 0)),
        scratch_shapes=[
            pltpu.VMEM(table.shape, F32),
            pltpu.VMEM((per_step // 2, LANES, LANES), F32),
            *LISTS,
        ],
        compiler_params=params(24),
        cost_estimate=pl.CostEstimate(flops=0, bytes_accessed=32 << 20, transcendentals=0),
        name="serve",
    )(asked, table)


AROUND = ((1, 0), (-1, 0), (1, 1), (1, -1), (-1, 1), (-1, -1), (0, 1), (0, -1))
X_SENDS, Y_SENDS = range(6), range(6, 8)


def rim_first(nx, ny, step):
    pairs = ny // 2
    late = step // (2 * pairs)
    at = step - 2 * pairs
    inner = nx - 2
    ends = at // (2 * inner)
    first = (step // pairs) * (nx - 1) * pairs + step % pairs
    end = (1 + at // 2) * pairs + (at % 2) * (pairs - 1)
    rest = at - 2 * inner
    middle = (1 + rest // (pairs - 2)) * pairs + 1 + rest % (pairs - 2)
    return (1 - late) * first + late * ((1 - ends) * end + ends * middle)


def rim_steps(nx, ny):
    return ny - 1, ny - 1 + 2 * (nx - 2)


class Rims:
    def __init__(self, sizes, out_ref, send_x, send_y, send_c, come_x, come_y, come_c, sent, come):
        self.sizes, self.out = sizes, out_ref
        self.at = (lax.axis_index("gx"), lax.axis_index("gy"))
        self.nx, self.ny = out_ref.shape[0] - 2, out_ref.shape[1] - 2
        self.cells = out_ref.shape[2]
        self.send, self.come = (send_x, send_y, send_c), (come_x, come_y, come_c)
        self.sems = (sent, come)

    def device(self, di, dj):
        (i, j), (size_x, size_y) = self.at, self.sizes
        return (lax.rem(i + di + size_x, size_x), lax.rem(j + dj + size_y, size_y))

    def copy(self, number):
        kind, at = (0, number) if number < 2 else (2, number - 2) if number < 6 else (1, number - 6)
        return pltpu.make_async_remote_copy(
            src_ref=self.send[kind].at[at],
            dst_ref=self.come[kind].at[at],
            send_sem=self.sems[0].at[number],
            recv_sem=self.sems[1].at[number],
            device_id=self.device(*AROUND[number]),
            device_id_type=MESH,
        )

    def greet(self):
        barrier = pltpu.get_barrier_semaphore()
        for di, dj in AROUND:
            pl.semaphore_signal(barrier, inc=1, device_id=self.device(di, dj), device_id_type=MESH)

    def send_first(self):
        pl.semaphore_wait(pltpu.get_barrier_semaphore(), len(AROUND))
        left = left_lanes(self.cells)
        deep = self.cells // 2
        for number in X_SENDS:
            di, dj = AROUND[number]
            x = self.nx if di > 0 else 1
            if dj == 0:
                for q in range(self.ny // 2):
                    self.send[0][number, q] = jnp.where(
                        left, self.out[x, 2 * q + 1], self.out[x, 2 * q + 2]
                    )
            else:
                row = self.out.at[x, self.ny if dj > 0 else 1]
                self.send[2][number - 2] = jnp.where(left[:deep], row[:deep, :], row[deep:, :])
            self.copy(number).start()

    def send_last(self):
        left = left_lanes(self.cells)
        for number in Y_SENDS:
            y = self.ny if AROUND[number][1] > 0 else 1
            for q in range(self.nx // 2):
                self.send[1][number - 6, q] = jnp.where(
                    left, self.out[2 * q + 1, y], self.out[2 * q + 2, y]
                )
            self.copy(number).start()

    def finish(self):
        left = left_lanes(self.cells)
        deep = self.cells // 2
        (i, j), (size_x, size_y) = self.at, self.sizes
        come_x, come_y, come_c = self.come

        def apart(both, keep):
            both = jnp.where(keep, both.astype(F32), 0.0)
            turned = pltpu.roll(both, LANES // 2, 1)
            side = left[: both.shape[0]]
            return (
                jnp.where(side, both, turned).astype(BF16),
                jnp.where(side, turned, both).astype(BF16),
            )

        for number, (di, dj) in enumerate(AROUND):
            self.copy(number).wait()
            keep_x = (i > 0) if di > 0 else (i < size_x - 1)
            keep_y = (j > 0) if dj > 0 else (j < size_y - 1)
            x = 0 if di > 0 else self.nx + 1
            y = 0 if dj > 0 else self.ny + 1
            if dj == 0:
                for q in range(self.ny // 2):
                    for p, row in enumerate(apart(come_x[number, q], keep_x)):
                        self.out[x, 2 * q + p + 1] = row
            elif di == 0:
                for q in range(self.nx // 2):
                    for p, row in enumerate(apart(come_y[number - 6, q], keep_y)):
                        self.out[2 * q + p + 1, y] = row
            else:
                place = self.out.at[x, y]
                for p, row in enumerate(apart(come_c[number - 2], keep_x & keep_y)):
                    place[p * deep : (p + 1) * deep, :] = row

    def around(self, step, work):
        first, last = rim_steps(self.nx, self.ny)

        @pl.when(step == 0)
        def _():
            self.greet()

        work()

        @pl.when(step == first)
        def _():
            self.send_first()

        @pl.when(step == last)
        def _():
            self.send_last()

        @pl.when(step == pl.num_programs(0) - 1)
        def _():
            self.finish()


def rim_scratch(nx, ny, cells):
    def buffers():
        return [
            pltpu.VMEM((2, ny // 2, cells, LANES), BF16),
            pltpu.VMEM((2, nx // 2, cells, LANES), BF16),
            pltpu.VMEM((4, cells // 2, LANES), BF16),
        ]

    return [*buffers(), *buffers(), pltpu.SemaphoreType.DMA((8,)), pltpu.SemaphoreType.DMA((8,))]


def column_of(row):
    return jnp.broadcast_to(row, (LANES, row.shape[1])).T


def collect_kernel(
    sizes,
    slot_ref,
    got_ref,
    share_ref,
    proj_ref,
    out_ref,
    table,
    stage,
    one_list,
    other_list,
    sems,
    *rim_refs,
):
    step = pl.program_id(0)
    nx, ny = out_ref.shape[0] - 2, out_ref.shape[1] - 2
    order = functools.partial(rim_first, nx, ny)
    pair = order(step)
    x, y = pair // (ny // 2), pair % (ny // 2) * 2
    half = got_ref.shape[0] * LANES
    cells = stage.shape[1]
    depth = CHUNK // cells

    @pl.when(step == 0)
    def _():
        left = left_lanes(LANES)

        def fill(owner, carry):
            at = pl.multiple_of(owner * LANES, LANES)
            rows = got_ref[owner].astype(F32)
            table[pl.ds(at, LANES), :] = jnp.where(left, rows, 0.0)
            table[pl.ds(half + at, LANES), :] = jnp.where(left, 0.0, rows)
            return carry

        lax.fori_loop(0, half // LANES, fill, 0, unroll=4)
        table[2 * half :, :] = jnp.zeros((8, LANES), F32)

    def gather(which, slot):
        for cell in range(cells):
            total = table[pl.ds(slot[cell], 1), :]
            for k in range(1, depth):
                total = total + table[pl.ds(slot[k * cells + cell], 1), :]
            stage[which, cell : cell + 1, :] = total
        total = stage[which]
        total = total + pltpu.roll(total, LANES // 2, 1)
        averaged = (total * column_of(share_ref[which])).astype(BF16)
        latent = jnp.dot(averaged, proj_ref[...], preferred_element_type=F32).astype(BF16)
        out_ref[x + 1, y + which + 1] = latent

    def work():
        chunks_of(slot_ref, (one_list, other_list), sems, step, gather, order)

    Rims(sizes, out_ref, *rim_refs).around(step, work)


def collect(sizes, nx, ny, slot, got, share, proj):
    strips, _, cells = share.shape
    half = got.shape[0] * LANES
    return pl.pallas_call(
        functools.partial(collect_kernel, sizes),
        grid=(strips // 2,),
        out_shape=jax.ShapeDtypeStruct((nx + 2, ny + 2, cells, LANES), BF16),
        in_specs=[
            whole(pl.ANY),
            whole(),
            pl.BlockSpec((2, 1, cells), lambda s: (rim_first(nx, ny, s), 0, 0)),
            whole(),
        ],
        out_specs=whole(),
        scratch_shapes=[
            pltpu.VMEM((2 * half + 8, LANES), F32),
            pltpu.VMEM((2, cells, LANES), F32),
            *LISTS,
            *rim_scratch(nx, ny, cells),
        ],
        compiler_params=params(36, collective_id=0, has_side_effects=True),
        name="collect",
    )(slot, got, share, proj)


def gelu_slope(value):
    inner = SCALE_ROOT * (value + CUBIC_TERM * value * value * value)
    tangent = jnp.tanh(inner)
    return 0.5 * (1.0 + tangent) + 0.5 * value * (1.0 - tangent * tangent) * SCALE_ROOT * (
        1.0 + 3.0 * CUBIC_TERM * value * value
    )


def taps_of(kernel):
    o, i = kernel.shape[:2]
    taps = kernel.transpose(2, 3, 1, 4, 0)
    taps = jnp.concatenate([taps, jnp.zeros((3, 1, i, 3, o), taps.dtype)], axis=1)
    order = [taps[..., c, :] for c in (1, 0, 2, 1)]
    return jnp.concatenate(order, axis=-1).reshape(12 * i, 4 * o)


def conv_strips(padded_ref, taps_ref, x, y):
    cells = padded_ref.shape[2]
    left = left_lanes(cells)
    strips = []
    for q in range(2):
        parts = []
        for a in range(3):
            parts.append(jnp.where(left, padded_ref[x + a, y + q], padded_ref[x + a, y + q + 1]))
            parts.append(padded_ref[x + a, y + q + 2])
        strips.append(jnp.concatenate(parts, axis=1))
    sums = jnp.dot(jnp.concatenate(strips, axis=0), taps_ref[...], preferred_element_type=F32)
    depth = lax.broadcasted_iota(I32, (cells, LANES), 0)
    results = []
    for q in range(2):
        one = sums[q * cells : (q + 1) * cells, :LANES]
        two = sums[q * cells : (q + 1) * cells, LANES:]
        below = jnp.where(depth == 0, 0.0, pltpu.roll(one, 1, 0))
        above = jnp.where(depth == cells - 1, 0.0, pltpu.roll(two, cells - 1, 0))
        sides = jnp.where(left, above, below)
        here = jnp.where(left, one, two)
        results.append(here + sides + pltpu.roll(sides, LANES // 2, 1))
    return results


def place_of(ny):
    first = 2 * pl.program_id(0)
    return first // ny, first % ny


def upstream_kernel(ny, padded_ref, taps_ref, out_ref):
    for q, strip in enumerate(conv_strips(padded_ref, taps_ref, *place_of(ny))):
        out_ref[q] = strip


def gate_kernel(sizes, padded_ref, taps_ref, upstream_ref, out_ref, *rim_refs):
    step = pl.program_id(0)
    nx, ny = out_ref.shape[0] - 2, out_ref.shape[1] - 2
    pair = rim_first(nx, ny, step)
    x, y = pair // (ny // 2), pair % (ny // 2) * 2

    def work():
        for q, preact in enumerate(conv_strips(padded_ref, taps_ref, x, y)):
            gated_grad = (upstream_ref[q] * gelu_slope(preact)).astype(BF16)
            out_ref[x + 1, y + q + 1] = gated_grad

    Rims(sizes, out_ref, *rim_refs).around(step, work)


def strip_spec(cells):
    return pl.BlockSpec((2, cells, LANES), lambda s: (s, 0, 0))


def conv_cost(strips, cells):
    return pl.CostEstimate(
        flops=2 * strips * cells * 12 * 64 * 4 * 64, bytes_accessed=12 << 20, transcendentals=0
    )


def upstream_of(padded, taps):
    nx, ny, cells = padded.shape[0] - 2, padded.shape[1] - 2, padded.shape[2]
    return pl.pallas_call(
        functools.partial(upstream_kernel, ny),
        grid=(nx * ny // 2,),
        out_shape=jax.ShapeDtypeStruct((nx * ny, cells, LANES), F32),
        in_specs=[whole(), whole()],
        out_specs=strip_spec(cells),
        compiler_params=params(24),
        cost_estimate=conv_cost(nx * ny, cells),
        name="upstream",
    )(padded, taps)


def gated(sizes, padded, taps, upstream):
    nx, ny, cells = padded.shape[0] - 2, padded.shape[1] - 2, padded.shape[2]
    return pl.pallas_call(
        functools.partial(gate_kernel, sizes),
        grid=(nx * ny // 2,),
        out_shape=jax.ShapeDtypeStruct(padded.shape, BF16),
        in_specs=[
            whole(),
            whole(),
            pl.BlockSpec((2, cells, LANES), lambda s: (rim_first(nx, ny, s), 0, 0)),
        ],
        out_specs=whole(),
        scratch_shapes=rim_scratch(nx, ny, cells),
        compiler_params=params(24, collective_id=1, has_side_effects=True),
        cost_estimate=conv_cost(nx * ny, cells),
        name="gated",
    )(padded, taps, upstream)


def spread_kernel(
    ny,
    slot_ref,
    padded_ref,
    taps_ref,
    proj_ref,
    share_ref,
    one_ref,
    two_ref,
    slots,
    stage,
    one_list,
    other_list,
    sems,
):
    step = pl.program_id(0)
    half = slots.shape[0] // 2 // LANES * LANES
    cells = stage.shape[1]
    depth = CHUNK // cells

    @pl.when(step == 0)
    def _():
        def clear(block, carry):
            slots[pl.ds(pl.multiple_of(block * 256, 256), 256), :] = jnp.zeros((256, LANES), F32)
            return carry

        lax.fori_loop(0, 2 * half // 256, clear, 0)

    for q, strip in enumerate(conv_strips(padded_ref, taps_ref, *place_of(ny))):
        projected = jnp.dot(strip.astype(BF16), proj_ref[...], preferred_element_type=F32)
        stage[q] = projected * column_of(share_ref[q])

    def lay(which, slot):
        for cell in range(cells):
            row = stage[which, cell : cell + 1, :]
            for k in range(depth):
                slots[pl.ds(slot[k * cells + cell], 1), :] = row

    chunks_of(slot_ref, (one_list, other_list), sems, step, lay)

    @pl.when(step == pl.num_programs(0) - 1)
    def _():
        left = left_lanes(LANES)

        def pack(owner, carry):
            at = pl.multiple_of(owner * LANES, LANES)
            both = jnp.where(left, slots[pl.ds(at, LANES), :], slots[pl.ds(half + at, LANES), :])
            both = both.astype(BF16)
            one_ref[owner] = both[:PART]
            two_ref[owner] = both[PART:]
            return carry

        lax.fori_loop(0, half // LANES, pack, 0, unroll=2)


def spread(slot, padded, taps, proj, share, half):
    nx, ny, cells = padded.shape[0] - 2, padded.shape[1] - 2, padded.shape[2]
    return pl.pallas_call(
        functools.partial(spread_kernel, ny),
        grid=(nx * ny // 2,),
        out_shape=(jax.ShapeDtypeStruct((half // LANES, PART, LANES), BF16),) * 2,
        in_specs=[
            whole(pl.ANY),
            whole(),
            whole(),
            whole(),
            pl.BlockSpec((2, 1, cells), lambda s: (s, 0, 0)),
        ],
        out_specs=(whole(), whole()),
        scratch_shapes=[
            pltpu.VMEM((2 * half + 8, LANES), F32),
            pltpu.VMEM((2, cells, LANES), F32),
            *LISTS,
        ],
        compiler_params=params(36),
        name="spread",
    )(slot, padded, taps, proj, share)


def add_rows(asked_ref, arrived_ref, sums, stage, lists, part):
    left = left_lanes()
    right = jnp.logical_not(left)

    def store(totals, places, values):
        for total, (one, two), (new_one, new_two) in zip(totals, places, values):
            pltpu.store(total.at[one, :], new_one, mask=left)
            pltpu.store(total.at[two, :], new_two, mask=right)

    def add(which, asked):
        waiting = None
        for block in range(CHUNK // (2 * LANES)):
            at = block * 2 * LANES + part * PART
            stage[block] = arrived_ref[which * (CHUNK // (2 * LANES)) + block].astype(F32)
            for group in range(PART // 2):
                totals = sums[:2] if group % 2 == 0 else sums[2:]
                places, values = [], []
                for total, row in zip(totals, (2 * group, 2 * group + 1)):
                    one, two = pl.ds(asked[at + row], 1), pl.ds(asked[at + row + LANES], 1)
                    value = stage[block, row : row + 1, :]
                    places.append((one, two))
                    values.append((total[one, :] + value, total[two, :] + value))
                if waiting is not None:
                    store(*waiting)
                waiting = (totals, places, values)
        store(*waiting)

    chunks_of(asked_ref, lists[:2], lists[2], pl.program_id(0), add)


def clear_sums(sums):
    def clear(block, carry):
        for total in sums:
            total[pl.ds(pl.multiple_of(block * LANES, LANES), LANES), :] = jnp.zeros(
                (LANES, LANES), F32
            )
        return carry

    lax.fori_loop(0, sums[0].shape[0] // LANES, clear, 0)


def first_kernel(asked_ref, arrived_ref, out_ref, one, two, three, stage, *lists):
    step = pl.program_id(0)
    sums = (out_ref, one, two, three)

    @pl.when(step == 0)
    def _():
        clear_sums(sums)

    add_rows(asked_ref, arrived_ref, sums, stage, lists, 0)

    @pl.when(step == pl.num_programs(0) - 1)
    def _():
        def finish(block, carry):
            rows = pl.ds(pl.multiple_of(block * LANES, LANES), LANES)
            out_ref[rows, :] = (out_ref[rows, :] + one[rows, :]) + (two[rows, :] + three[rows, :])
            return carry

        lax.fori_loop(0, out_ref.shape[0] // LANES, finish, 0)


def last_kernel(asked_ref, arrived_ref, before_ref, out_ref, *scratch):
    sums, (held, sem, stage, *lists) = scratch[:4], scratch[4:]
    step = pl.program_id(0)
    points = out_ref.shape[1]

    def fetch():
        return pltpu.make_async_copy(before_ref, held, sem)

    @pl.when(step == 0)
    def _():
        fetch().start()
        clear_sums(sums)

    add_rows(asked_ref, arrived_ref, sums, stage, lists, 1)

    @pl.when(step == pl.num_programs(0) - 1)
    def _():
        fetch().wait()

        def finish(block, carry):
            at = pl.multiple_of(block * LANES, LANES)
            rows = pl.ds(SPARE + at, LANES)
            total = held[rows, :]
            for other in sums:
                total = total + other[rows, :]
            turned = total.T
            out_ref[:, pl.ds(at, LANES)] = turned[: LANES // 2] + turned[LANES // 2 :]
            return carry

        lax.fori_loop(0, points // LANES, finish, 0, unroll=8)


def settle_specs(arrived):
    per_step = 2 * CHUNK // (2 * LANES)
    grid = (arrived.shape[0] // per_step,)
    specs = [whole(pl.ANY), pl.BlockSpec((per_step, PART, LANES), lambda s: (s, 0, 0))]
    return grid, specs, [pltpu.VMEM((per_step // 2, PART, LANES), F32), *LISTS]


def settle_first(asked, arrived, points):
    grid, specs, scratch = settle_specs(arrived)
    return pl.pallas_call(
        first_kernel,
        grid=grid,
        out_shape=jax.ShapeDtypeStruct((SPARE + points, LANES), F32),
        in_specs=specs,
        out_specs=whole(),
        scratch_shapes=[pltpu.VMEM((SPARE + points, LANES), F32)] * 3 + scratch,
        compiler_params=params(44),
        cost_estimate=pl.CostEstimate(flops=0, bytes_accessed=64 << 20, transcendentals=0),
        name="settle_first",
    )(asked, arrived)


def settle_last(asked, arrived, before, points):
    grid, specs, scratch = settle_specs(arrived)
    return pl.pallas_call(
        last_kernel,
        grid=grid,
        out_shape=jax.ShapeDtypeStruct((LANES // 2, points), F32),
        in_specs=[*specs, whole(pl.ANY)],
        out_specs=whole(),
        scratch_shapes=[pltpu.VMEM((SPARE + points, LANES), F32)] * 5
        + [pltpu.SemaphoreType.DMA(())]
        + scratch,
        compiler_params=params(56),
        name="settle_last",
    )(asked, arrived, before)


def rims_of(shard, axis, dim):
    size, length = lax.axis_size(axis), shard.shape[dim]
    up = [(i, i + 1) for i in range(size - 1)]
    down = [(j, i) for i, j in up]
    before = lax.ppermute(lax.slice_in_dim(shard, length - 1, length, axis=dim), axis, up)
    after = lax.ppermute(lax.slice_in_dim(shard, 0, 1, axis=dim), axis, down)
    return before, after


def twice(matrix):
    wide = jnp.concatenate([matrix, matrix], axis=1)
    return jnp.concatenate([wide, jnp.zeros_like(wide)], axis=0)


def flipped(kernel):
    return jnp.flip(kernel, (2, 3, 4)).transpose(1, 0, 2, 3, 4)


def shards(
    point_features, neighbour_rows, neighbour_owner, valid, proj, kernel_one, kernel_two, cotangent
):
    channels, points = point_features.shape
    depth, nx, ny, cells = neighbour_rows.shape
    strips = nx * ny
    size_x, size_y = lax.axis_size("gx"), lax.axis_size("gy")
    devices = size_x * size_y
    cap = depth * strips * cells // devices
    half = devices * LANES

    def swap(array):
        return lax.all_to_all(array, ("gx", "gy"), split_axis=0, concat_axis=0, tiled=True)

    flat = (depth * strips, cells)
    slot, wanted = route(
        neighbour_owner.reshape(flat), neighbour_rows.reshape(flat), valid.reshape(flat), strips, devices, cap
    )
    slot = slot.reshape(-1)
    used = jnp.sum(valid.reshape(depth, strips, 1, cells), axis=0)
    share = 1.0 / jnp.maximum(used, 1).astype(F32)

    x_rims = rims_of(cotangent, "gx", 1)
    wanted, x_rims = lax.optimization_barrier((wanted, x_rims))
    asked = swap(wanted).reshape(-1)
    table = table_of(point_features)
    served = serve(asked, table)
    low, high = (
        jnp.concatenate([part[:, :, at : at + 1] for part in (x_rims[0], cotangent, x_rims[1])], 1)
        for at in (0, ny - 1)
    )
    y_rims = rims_of(jnp.concatenate([low, high], axis=2), "gy", 2)
    served, y_rims = lax.optimization_barrier((served, y_rims))
    got = swap(served)

    upward = jnp.concatenate([x_rims[0], cotangent, x_rims[1]], axis=1)
    upward = jnp.concatenate([y_rims[0], upward, y_rims[1]], axis=2)
    upward = upward.transpose(1, 2, 3, 0)
    upward = jnp.concatenate([upward, upward], axis=-1)
    upstream = upstream_of(upward, taps_of(flipped(kernel_two)))

    sizes = (size_x, size_y)
    latent = collect(sizes, nx, ny, slot, got, share, twice(proj))
    gated_grad = gated(sizes, latent, taps_of(kernel_one), upstream)
    one, two = spread(slot, gated_grad, taps_of(flipped(kernel_one)), twice(proj.T), share, half)
    one = swap(one)
    one, two = lax.optimization_barrier((one, two))
    two = swap(two)
    return settle_last(asked, two, settle_first(asked, one, points), points)


def solution(mesh):
    placed = (
        P(None, ("gx", "gy")),
        P(None, "gx", "gy", None),
        P(None, "gx", "gy", None),
        P(None, "gx", "gy", None),
        P(),
        P(),
        P(),
        P(None, "gx", "gy", None),
    )
    return jax.shard_map(
        shards, mesh=mesh, in_specs=placed, out_specs=P(None, ("gx", "gy")), check_vma=False
    )
```
